256 devices in a mesh: member: 8 (over y, core), grid: 32 (over x, z).
Axes of the slice: x: 4, y: 4, z: 8, core: 2. Of those that a mesh axis runs over, the one named last changes fastest.
Arguments:
- prediction: float32 [8, 100, 131072], P('member', None, 'grid'), may hold values from -6 to 6
- reference_state: float32 [100, 131072], P(None, 'grid'), may hold values from -6 to 6
- quantity_penalty_factor: float32 [100], replicated, may hold values from 0.1 to 1
- point_surface_factor: float32 [131072], P('grid'), may hold values from 0.1 to 3
- latitude_row_start: int32 [33], replicated, may hold values from 0 to 65536, as said below
Outputs:
- scaled_derivative: float32 [8, 100, 65536], P('member', None, 'grid')
- loss: float32 [], replicated
The draws below stay inside these ranges and needn't reach their ends.
Inputs may be any that keep to these rules, and one draw needn't show every extreme that they name: latitude_row_start[0] = 0, latitude_row_start[32] = 65536, and latitude_row_start[g] differs from g * 2048 by at most 1023; every band holds 2 to 4094 cells, and some band holds exactly 4094.
All inputs are finite; a program needn't handle non-finite values.
Results may differ from the reference program's by a relative error of at most 0.0003.
Values sent between devices are 32-bit elements; how exact they have to be, the bound alone decides.
A program may use at most 64 MiB of HBM per device.

```python
import math
import jax
import jax.numpy as jnp
from jax import lax

QUANTITY_NUMBER = 100
E = 2048
ENSEMBLE_SIZE = 8
CAP = 4096
CELLS = 65536
GRID_POINT_ROOM = 131072
N_GRID = 32


def draw_point_surface_factor(key, part):
    key = jax.random.fold_in(key, 11)
    rising = 1.0 + 2.0 * jnp.arange(GRID_POINT_ROOM, dtype=jnp.float32) / GRID_POINT_ROOM
    rough = jnp.exp(jax.random.uniform(key, (GRID_POINT_ROOM,), jnp.float32, jnp.log(0.1), 0.0))
    return rough * rising


def draw_latitude_row_start(key, part):
    key = jax.random.fold_in(key, 7)
    first_key, second_key = jax.random.split(key)
    half_span = E // 2 - 1
    shifts = jax.random.randint(first_key, (N_GRID - 1,), -half_span, half_span + 1)
    place = jax.random.randint(second_key, (), 0, N_GRID - 2)
    shifts = shifts.at[place].set(-half_span).at[place + 1].set(half_span)
    padded = jnp.concatenate([jnp.zeros((1,), jnp.int32), shifts.astype(jnp.int32), jnp.zeros((1,), jnp.int32)])
    return (jnp.arange(N_GRID + 1, dtype=jnp.int32) * E + padded).astype(jnp.int32)


def steps_of(own_key, dims, pieces, low, high):
    def one(axis_at, parts):
        heights = jax.random.uniform(jax.random.fold_in(jax.random.fold_in(own_key, 6), axis_at), (parts,), jnp.float32, low / len(pieces), high / len(pieces))
        return jnp.repeat(jnp.exp(heights), dims[axis_at] // parts).reshape((-1,) + (1,) * (len(dims) - axis_at - 1))

    level = one(*pieces[0])
    for cut in pieces[1:]:
        level = level * one(*cut)
    return level


def gaussian(rng, shape, width, limit, cuts=(), kind=jnp.bfloat16):
    values = width * jax.random.normal(rng, shape, jnp.float32)
    if cuts:
        values = values * steps_of(rng, shape, cuts, -0.22, 0.18)
    return jnp.clip(values, -limit, limit).astype(kind)


def setup_inputs(seed: int = 0) -> dict:
    seeds = jax.random.split(jax.random.key(seed), 6)
    prediction = gaussian(seeds[0], (ENSEMBLE_SIZE, QUANTITY_NUMBER, GRID_POINT_ROOM), 1.0, 6.0, ((0, 8), (2, 32)), jnp.float32)
    reference_state = gaussian(seeds[1], (QUANTITY_NUMBER, GRID_POINT_ROOM), 1.0, 6.0, ((1, 32),), jnp.float32)
    quantity_penalty_factor = jnp.clip(jnp.exp(jax.random.uniform(seeds[2], (QUANTITY_NUMBER,), jnp.float32, math.log(0.1), math.log(1.0))), 0.1, 1.0)
    point_surface_factor = draw_point_surface_factor(jax.random.fold_in(seeds[5], 71), 0)
    latitude_row_start = draw_latitude_row_start(jax.random.fold_in(seeds[5], 71), 0)
    return dict(prediction=prediction, reference_state=reference_state, quantity_penalty_factor=quantity_penalty_factor, point_surface_factor=point_surface_factor, latitude_row_start=latitude_row_start)


def reference(prediction, reference_state, quantity_penalty_factor, point_surface_factor, latitude_row_start):
    cell_ids = jnp.arange(CELLS, dtype=jnp.int32)
    band_of = lax.optimization_barrier(jnp.sum((cell_ids[:, None] >= latitude_row_start[None, 1:N_GRID]).astype(jnp.int32), axis=1)).astype(jnp.int32)
    point_positions = (band_of * CAP + cell_ids - latitude_row_start[band_of]).astype(jnp.int32)
    prediction_arrays = jnp.take(prediction, point_positions, axis=2)
    receiver = jnp.take(reference_state, point_positions, axis=1)
    factors = quantity_penalty_factor[:, None] * jnp.take(point_surface_factor, point_positions)[None, :]
    scale = 1.0 / (QUANTITY_NUMBER * CELLS)
    analysis_accumulated = lax.optimization_barrier(jnp.sum(factors[None] * (prediction_arrays - receiver[None]) ** 2, axis=(1, 2)))
    columns = []
    for partner in range(ENSEMBLE_SIZE):
        deviation = prediction_arrays - prediction_arrays[partner][None]
        columns.append(lax.optimization_barrier(jnp.sum(factors[None] * deviation * deviation, axis=(1, 2))))
    pair_sum = jnp.stack(columns, axis=1)
    analysis_distance = jnp.sqrt(analysis_accumulated * scale + 1e-06)
    pair_dist = jnp.sqrt(pair_sum * scale + 1e-06)
    offdiag = 1.0 - jnp.eye(ENSEMBLE_SIZE, dtype=jnp.float32)
    reciprocal = offdiag / pair_dist
    loss = jnp.sum(analysis_distance) / ENSEMBLE_SIZE - jnp.sum(offdiag * pair_dist) / (2.0 * ENSEMBLE_SIZE * (ENSEMBLE_SIZE - 1))
    blended = jnp.einsum('ls,shp->lhp', reciprocal, prediction_arrays, precision=lax.Precision.HIGHEST)
    dispersion = prediction_arrays * lax.optimization_barrier(jnp.sum(reciprocal, axis=1))[:, None, None] - blended
    scaled_derivative = factors[None] * ((prediction_arrays - receiver[None]) / analysis_distance[:, None, None] - dispersion / (ENSEMBLE_SIZE - 1))
    return (scaled_derivative, loss)
```

```python
import functools

import jax
import jax.numpy as jnp
from jax import lax
from jax.experimental import pallas as pl
from jax.experimental.pallas import tpu as pltpu
from jax.sharding import PartitionSpec as P

MESH = pl.DeviceIdType.MESH
F32 = jnp.float32
LANES = 128
CHUNKS = ((0, 5), (5, 11), (11, 18), (18, 25))
NX, NZ = 4, 8
NY, NC = 4, 2
MEMBERS = 8
GRID = 32
GROUPS = MEMBERS // 2
PAIRS = [(a, b) for a in range(MEMBERS) for b in range(a + 1, MEMBERS)]
ENTRIES = MEMBERS + len(PAIRS)


def align_kernel(
    starts,
    pred,
    truth,
    area,
    edge_out,
    own,
    y_out,
    y_own,
    xin,
    yin,
    win,
    edges,
    parts,
    y_edge,
    y_part,
    load_sem,
    save_sem,
):
    groups, share, tiles = pred.shape[:3]
    rows = groups * share
    edge = 8 * LANES
    half = 2 * edge
    lead = xin.shape[2] - tiles
    chunks = len(CHUNKS)
    m = lax.axis_index("member")
    g = lax.axis_index("grid")
    side, group = m // GROUPS, m % GROUPS
    row0 = group * share
    full = rows // 8 * 8
    spread = y_part.shape[0] // 8 - 1
    y_at = pl.multiple_of(group * 8, 8)
    y_span = share * 8 + 8

    x_loads = [
        pltpu.make_async_copy(
            pred.at[:, pl.ds(lo, hi - lo)],
            xin.at[:, pl.ds(lo, hi - lo), pl.ds(lead, tiles)],
            load_sem.at[c],
        )
        for c, (lo, hi) in enumerate(CHUNKS)
    ]
    y_load = pltpu.make_async_copy(truth, yin, load_sem.at[chunks])
    w_load = pltpu.make_async_copy(area, win.at[pl.ds(lead, tiles)], load_sem.at[chunks + 1])
    for copy in x_loads + [y_load, w_load]:
        copy.start()

    lo_cell = starts[g] - g * half
    shift = lo_cell + edge
    whole = lax.div(shift, LANES)
    part = lax.rem(shift, LANES)
    lane = lax.broadcasted_iota(jnp.int32, (8, LANES), 1)
    from_before = lane >= LANES - part

    def turned(now, before):
        return pltpu.roll(jnp.where(from_before, before, now), part, 1)

    def aligned(k, n, eighth):
        at = lead + 8 * eighth - whole
        return turned(xin[k, n, pl.ds(at, 8), :], xin[k, n, pl.ds(at - 1, 8), :])

    def aligned_area(eighth):
        at = lead + 8 * eighth - whole
        return turned(win[pl.ds(at, 8), :], win[pl.ds(at - 1, 8), :])

    def aligned_truth(eighth, put):
        for n in range(0, spread, 8):
            r = pl.multiple_of(jnp.minimum(row0 - group + n, full - 8), 8)

            def tile(t):
                at = lax.rem(8 * eighth + t - whole + 2 * tiles, tiles) * LANES
                cols = pl.ds(pl.multiple_of(at, LANES), LANES)
                value = yin[pl.ds(r, 8), cols]
                if n + 8 < spread:
                    return value
                rest = jnp.zeros((8 + full - rows, LANES), F32)
                tail = jnp.concatenate([yin[pl.ds(full, rows - full), cols], rest], axis=0)
                return jnp.where(group == GROUPS - 1, tail, value)

            before = tile(-1)
            for t in range(8):
                now = tile(t)
                put(n, t, turned(now, before))
                before = now

    saves = []
    for c, (lo, hi) in enumerate(CHUNKS):
        x_loads[c].wait()

        def align(n, _):
            for k in range(GROUPS):
                edges[k, n] = aligned(k, n, 3)
                edges[GROUPS + k, n] = aligned(k, n, 0)
                parts[k, n] = aligned(k, n, 1)
                parts[GROUPS + k, n] = aligned(k, n, 2)
            return 0

        lax.fori_loop(lo, hi, align, 0)
        for i, (src, dst) in enumerate(((edges, edge_out), (parts, own))):
            run = (slice(None), pl.ds(lo, hi - lo))
            saves.append(pltpu.make_async_copy(src.at[run], dst.at[run], save_sem.at[2 * c + i]))
            saves[-1].start()

    y_load.wait()
    w_load.wait()
    for i, (src, dst, eighth) in enumerate(((y_edge, y_out, 3 - 3 * side), (y_part, y_own, 1 + side))):

        def put(n, t, value):
            src[pl.ds(n * 8 + t, 8, stride=8), :] = value

        aligned_truth(eighth, put)
        src[pl.ds(y_at + share * 8, 8), :] = aligned_area(eighth)
        saves.append(
            pltpu.make_async_copy(src.at[pl.ds(y_at, y_span)], dst, save_sem.at[2 * chunks + i])
        )
        saves[-1].start()
    for copy in saves:
        copy.wait()


def exchange_kernel(
    starts,
    penalty,
    edge_out,
    own,
    y_out,
    truth,
    out,
    loss,
    edge_in,
    parts,
    xs,
    y_in,
    y_own,
    result,
    first,
    second,
    coef,
    load_sem,
    edge_send,
    edge_recv,
    y_send,
    y_recv,
    part_send,
    part_recv,
    own_sem,
    first_send,
    first_recv,
    second_send,
    second_recv,
    res_send,
    res_recv,
    keep_sem,
):
    share = parts.shape[1]
    rows = share * GROUPS
    edge = 8 * LANES
    half = 2 * edge
    m = lax.axis_index("member")
    g = lax.axis_index("grid")
    my, mc = m // NC, m % NC
    gx, gz = g // NZ, g % NZ
    side, group = m // GROUPS, m % GROUPS
    row0 = group * share

    def member_peer(p):
        return {"member": (m + p) % MEMBERS, "grid": g}

    def grid_peer(step):
        return {"member": m, "grid": (g + step + GRID) % GRID}

    def first_peer(p):
        return {"member": ((my + p // NX) % NY) * NC + mc, "grid": ((gx + p % NX) % NX) * NZ + gz}

    def second_peer(p):
        return {"member": my * NC + (mc + p % NC) % NC, "grid": gx * NZ + (gz + p // NC) % NZ}

    part_loads = [
        pltpu.make_async_copy(
            own.at[:, pl.ds(lo, hi - lo)], parts.at[:, pl.ds(lo, hi - lo)], load_sem.at[c]
        )
        for c, (lo, hi) in enumerate(CHUNKS)
    ]
    y_load = pltpu.make_async_copy(truth, y_own, load_sem.at[len(CHUNKS)])
    for copy in part_loads + [y_load]:
        copy.start()

    peers = [member_peer(p) for p in range(1, MEMBERS)]
    peers += [grid_peer(1), grid_peer(-1)]
    peers += [first_peer(p) for p in range(1, NX * NY)]
    peers += [second_peer(p) for p in range(1, NZ * NC)]
    barrier = pltpu.get_barrier_semaphore()
    for peer in peers:
        pl.semaphore_signal(barrier, inc=1, device_id=peer, device_id_type=MESH)

    lo_cell = starts[g] - g * half
    hi_cell = starts[g + 1] - g * half
    lane = lax.broadcasted_iota(jnp.int32, (8, LANES), 1)
    sub = lax.broadcasted_iota(jnp.int32, (8, LANES), 0)

    def edge_copy(c, s):
        lo, hi = CHUNKS[c]
        where = (pl.ds(s * GROUPS, GROUPS), pl.ds(lo, hi - lo))
        return pltpu.make_async_remote_copy(
            src_ref=edge_out.at[where],
            dst_ref=edge_in.at[where],
            send_sem=edge_send.at[c, s],
            recv_sem=edge_recv.at[c, s],
            device_id=grid_peer(1 if s == 0 else -1),
            device_id_type=MESH,
        )

    y_copy = pltpu.make_async_remote_copy(
        src_ref=y_out,
        dst_ref=y_in,
        send_sem=y_send,
        recv_sem=y_recv,
        device_id={"member": m, "grid": (g + 1 + side * (GRID - 2)) % GRID},
        device_id_type=MESH,
    )

    pl.semaphore_wait(barrier, len(peers))
    for c in range(len(CHUNKS)):
        for s in range(2):
            edge_copy(c, s).start()
        if c == 0:
            y_copy.start()

    def part_copy(c, p):
        lo, hi = CHUNKS[c]
        peer = member_peer(p)
        return pltpu.make_async_remote_copy(
            src_ref=parts.at[peer["member"], pl.ds(lo, hi - lo)],
            dst_ref=xs.at[m, pl.ds(lo, hi - lo)],
            send_sem=part_send.at[c, p],
            recv_sem=part_recv.at[c, p],
            device_id=peer,
            device_id_type=MESH,
        )

    def own_copy(c):
        lo, hi = CHUNKS[c]
        return pltpu.make_async_copy(
            parts.at[m, pl.ds(lo, hi - lo)], xs.at[m, pl.ds(lo, hi - lo)], own_sem.at[c]
        )

    def owned(s):
        cell = s * edge + sub * LANES + lane
        return (cell >= lo_cell) & (cell < hi_cell)

    in_half = [owned(0), owned(1)]
    for c, (lo, hi) in enumerate(CHUNKS):
        part_loads[c].wait()
        for s in range(2):
            edge_copy(c, s).wait_recv()

        def merge(n, _):
            for k in range(MEMBERS):
                parts[k, n] = jnp.where(in_half[k // GROUPS], parts[k, n], edge_in[k, n])
            return 0

        lax.fori_loop(lo, hi, merge, 0)
        for p in range(1, MEMBERS):
            part_copy(c, p).start()
        own_copy(c).start()

    y_load.wait()
    y_copy.wait_recv()
    in_own = owned(side)

    def merge_truth(n, _):
        at = pl.ds(pl.multiple_of(n * 8, 8), 8)
        y_own[at, :] = jnp.where(in_own, y_own[at, :], y_in[at, :])
        return 0

    lax.fori_loop(0, share + 1, merge_truth, 0)
    own_area = y_own[pl.ds(share * 8, 8), :]

    def load_row(n):
        x = [xs[k, n] for k in range(MEMBERS)]
        y = y_own[pl.ds(pl.multiple_of(n * 8, 8), 8), :]
        return x, y, penalty[row0 + n] * own_area

    sums = (jnp.zeros((8, LANES), F32),) * ENTRIES
    for c, (lo, hi) in enumerate(CHUNKS):
        own_copy(c).wait()
        for p in range(1, MEMBERS):
            part_copy(c, p).wait_recv()

        def add(n, sums):
            sums = list(sums)
            x, y, lw = load_row(n)
            for k in range(MEMBERS):
                d = x[k] - y
                sums[k] = sums[k] + lw * d * d
            for e, (a, b) in enumerate(PAIRS):
                d = x[a] - x[b]
                sums[MEMBERS + e] = sums[MEMBERS + e] + lw * d * d
            return tuple(sums)

        sums = lax.fori_loop(lo, hi, add, sums)

    message = jnp.zeros((8, LANES), F32)
    for e in range(0, ENTRIES, 8):
        column = [jnp.sum(s, axis=0, keepdims=True) for s in sums[e : e + 8]]
        column += [jnp.zeros((1, LANES), F32)] * (8 - len(column))
        total = jnp.sum(jnp.concatenate(column, axis=0), axis=1, keepdims=True)
        message = jnp.where(lane == e // 8, total, message)

    def exchange(message, buffer, send, recv, peer_of, count, place):
        buffer[place] = message
        copies = [
            pltpu.make_async_remote_copy(
                src_ref=buffer.at[place],
                dst_ref=buffer.at[place],
                send_sem=send.at[p],
                recv_sem=recv.at[p],
                device_id=peer_of(p),
                device_id_type=MESH,
            )
            for p in range(1, count)
        ]
        for copy in copies:
            copy.start()
        for copy in copies:
            copy.wait_recv()
        total = buffer[0]
        for i in range(1, count):
            total = total + buffer[i]
        return total, copies

    message, first_copies = exchange(
        message, first, first_send, first_recv, first_peer, NX * NY, my * NX + gx
    )
    message, second_copies = exchange(
        message, second, second_send, second_recv, second_peer, NZ * NC, gz * NC + mc
    )

    scale = 1.0 / (rows * half * GRID)
    distance = jnp.sqrt(message * scale + 1e-06)
    entry = lane * 8 + sub
    is_truth = entry < MEMBERS
    share_of = jnp.where(is_truth, 1.0 / MEMBERS, -1.0 / (MEMBERS * (MEMBERS - 1)))
    loss[...] = jnp.sum(jnp.where(entry < ENTRIES, distance * share_of, 0.0), keepdims=True)
    factor = jnp.where(is_truth, 1.0, 1.0 / (MEMBERS - 1)) / distance
    for e in range(ENTRIES):
        coef[e] = jnp.broadcast_to(factor[e % 8 : e % 8 + 1, e // 8 : e // 8 + 1], (8, LANES))

    def place_of(c):
        lo, hi = CHUNKS[c]
        return out.at[pl.ds(row0 + lo, hi - lo), pl.ds(pl.multiple_of(side * 8, 8), 8)]

    def res_copy(c, p):
        lo, hi = CHUNKS[c]
        peer = member_peer(p)
        return pltpu.make_async_remote_copy(
            src_ref=result.at[peer["member"], pl.ds(lo, hi - lo)],
            dst_ref=place_of(c),
            send_sem=res_send.at[c, p],
            recv_sem=res_recv.at[c, p],
            device_id=peer,
            device_id_type=MESH,
        )

    def keep_copy(c):
        lo, hi = CHUNKS[c]
        return pltpu.make_async_copy(
            result.at[m, pl.ds(lo, hi - lo)], place_of(c), keep_sem.at[c]
        )

    for c, (lo, hi) in enumerate(CHUNKS):

        def derive(n, _):
            x, y, lw = load_row(n)
            o = [(x[k] - y) * coef[k] for k in range(MEMBERS)]
            for e, (a, b) in enumerate(PAIRS):
                d = (x[a] - x[b]) * coef[MEMBERS + e]
                o[a] = o[a] - d
                o[b] = o[b] + d
            for k in range(MEMBERS):
                result[k, n] = lw * o[k]
            return 0

        lax.fori_loop(lo, hi, derive, 0)
        for p in range(1, MEMBERS):
            res_copy(c, p).start()
        keep_copy(c).start()

    for c in range(len(CHUNKS)):
        for s in range(2):
            edge_copy(c, s).wait_send()
        for p in range(1, MEMBERS):
            part_copy(c, p).wait_send()
    y_copy.wait_send()
    for copy in first_copies + second_copies:
        copy.wait_send()
    for c in range(len(CHUNKS)):
        keep_copy(c).wait()
        for p in range(1, MEMBERS):
            res_copy(c, p).wait_send()
            res_copy(c, p).wait_recv()


def local(prediction, reference_state, penalty, area, starts):
    rows, slots = prediction.shape[1:]
    tiles = slots // LANES
    share = rows // GROUPS
    spread = -(-(share + GROUPS - 1) // 8) * 8
    lead = tiles // 2 + 8
    chunks = len(CHUNKS)
    vmem = functools.partial(pltpu.VMEM, dtype=F32)
    array = functools.partial(jax.ShapeDtypeStruct, dtype=F32)
    dma = pltpu.SemaphoreType.DMA
    in_smem = pl.BlockSpec(memory_space=pltpu.SMEM)
    anywhere = pl.BlockSpec(memory_space=pl.ANY)
    fields = (MEMBERS, share, 8, LANES)
    y_share = (share * 8 + 8, LANES)
    y_spread = (spread * 8 + 8, LANES)
    aligned = pl.pallas_call(
        align_kernel,
        name="align",
        out_shape=(array(fields), array(fields), array(y_share), array(y_share)),
        in_specs=[in_smem, anywhere, anywhere, anywhere],
        out_specs=(anywhere,) * 4,
        scratch_shapes=[
            vmem((GROUPS, share, tiles + lead, LANES)),
            vmem((rows, slots)),
            vmem((tiles + lead, LANES)),
            vmem(fields),
            vmem(fields),
            vmem(y_spread),
            vmem(y_spread),
            dma((chunks + 2,)),
            dma((2 * chunks + 2,)),
        ],
        compiler_params=pltpu.CompilerParams(vmem_limit_bytes=40 * 2**20),
    )(
        starts,
        prediction.reshape(GROUPS, share, tiles, LANES),
        reference_state,
        area.reshape(tiles, LANES),
    )
    result, loss = pl.pallas_call(
        exchange_kernel,
        name="energy_score",
        out_shape=(array((rows, tiles // 2, LANES)), array((1, 1))),
        in_specs=[in_smem, in_smem] + [anywhere] * 4,
        out_specs=(anywhere, pl.BlockSpec(memory_space=pltpu.VMEM)),
        scratch_shapes=[
            vmem(fields),
            vmem(fields),
            vmem(fields),
            vmem(y_share),
            vmem(y_share),
            vmem(fields),
            vmem((NX * NY, 8, LANES)),
            vmem((NZ * NC, 8, LANES)),
            vmem((ENTRIES, 8, LANES)),
            dma((chunks + 1,)),
            dma((chunks, 2)),
            dma((chunks, 2)),
            dma,
            dma,
            dma((chunks, MEMBERS)),
            dma((chunks, MEMBERS)),
            dma((chunks,)),
            dma((NX * NY,)),
            dma((NX * NY,)),
            dma((NZ * NC,)),
            dma((NZ * NC,)),
            dma((chunks, MEMBERS)),
            dma((chunks, MEMBERS)),
            dma((chunks,)),
        ],
        compiler_params=pltpu.CompilerParams(
            collective_id=0, has_side_effects=True, vmem_limit_bytes=40 * 2**20
        ),
    )(starts, penalty, *aligned)
    return (result.reshape(1, rows, slots // 2), loss.reshape(()))


def solution(mesh):
    placed = (P("member", None, "grid"), P(None, "grid"), P(), P("grid"), P())
    return jax.shard_map(
        local,
        mesh=mesh,
        in_specs=placed,
        out_specs=(P("member", None, "grid"), P()),
        check_vma=False,
    )
```

```python
import functools

import jax
import jax.numpy as jnp
from jax import lax
from jax.experimental import pallas as pl
from jax.experimental.pallas import tpu as pltpu
from jax.sharding import PartitionSpec as P

MESH = pl.DeviceIdType.MESH
F32 = jnp.float32
LANES = 128
VMEM_BYTES = 62 * 2**20
CHUNKS = ((0, 5), (5, 10), (10, 15), (15, 20), (20, 25))
RETURNS = ((0, 3), (3, 12), (12, 25))
NX, NZ = 4, 8
NY, NC = 4, 2
MEMBERS = 8
GRID = 32
GROUPS = MEMBERS // 2
PAIRS = [(a, b) for a in range(MEMBERS) for b in range(a + 1, MEMBERS)]
ENTRIES = MEMBERS + len(PAIRS)


def kernel(
    starts,
    penalty,
    pred,
    truth,
    area,
    out,
    loss,
    xin,
    yin,
    win,
    y_rows,
    edge_out,
    edge_in,
    parts,
    xs,
    y_out,
    y_in,
    y_own,
    result,
    first,
    second,
    coef,
    load_sem,
    edge_send,
    edge_recv,
    y_send,
    y_recv,
    part_send,
    part_recv,
    own_sem,
    first_send,
    first_recv,
    second_send,
    second_recv,
    res_send,
    res_recv,
    keep_sem,
):
    share, tiles = pred.shape[1], pred.shape[2]
    rows = share * GROUPS
    edge = tiles // 4 * LANES
    half = 2 * edge
    chunks = len(CHUNKS)
    m = lax.axis_index("member")
    g = lax.axis_index("grid")
    my, mc = m // NC, m % NC
    gx, gz = g // NZ, g % NZ
    side, group = m // GROUPS, m % GROUPS
    row0 = group * share

    def member_peer(p):
        return {"member": (m + p) % MEMBERS, "grid": g}

    def grid_peer(step):
        return {"member": m, "grid": (g + step + GRID) % GRID}

    def first_peer(p):
        return {"member": ((my + p // NX) % NY) * NC + mc, "grid": ((gx + p % NX) % NX) * NZ + gz}

    def second_peer(p):
        return {"member": my * NC + (mc + p % NC) % NC, "grid": gx * NZ + (gz + p // NC) % NZ}

    x_loads = [
        pltpu.make_async_copy(
            pred.at[:, pl.ds(lo, hi - lo)], xin.at[:, pl.ds(lo, hi - lo)], load_sem.at[c]
        )
        for c, (lo, hi) in enumerate(CHUNKS)
    ]
    y_load = pltpu.make_async_copy(truth, yin, load_sem.at[chunks])
    w_load = pltpu.make_async_copy(area, win, load_sem.at[chunks + 1])
    for copy in x_loads + [y_load, w_load]:
        copy.start()

    peers = [member_peer(p) for p in range(1, MEMBERS)]
    peers += [grid_peer(1), grid_peer(-1)]
    peers += [first_peer(p) for p in range(1, NX * NY) if p % NX]
    peers += [second_peer(p) for p in range(NC, NZ * NC)]
    barrier = pltpu.get_barrier_semaphore()
    for peer in peers:
        pl.semaphore_signal(barrier, inc=1, device_id=peer, device_id_type=MESH)

    lo_cell = starts[g] - g * half
    hi_cell = starts[g + 1] - g * half
    shift = lo_cell + edge
    whole = lax.div(shift, LANES)
    part = lax.rem(shift, LANES)
    lane = lax.broadcasted_iota(jnp.int32, (8, LANES), 1)
    wrapped = lax.broadcasted_iota(jnp.int32, (tiles, LANES), 1) >= LANES - part

    def aligned(row):
        now = pltpu.roll(row, whole, 0)
        row = pltpu.roll(jnp.where(wrapped, pltpu.roll(now, 1, 0), now), part, 1)
        return [row[i : i + 8] for i in range(0, tiles, 8)]

    sub = lax.broadcasted_iota(jnp.int32, (8, LANES), 0)

    def edge_copy(c, s):
        lo, hi = CHUNKS[c]
        where = (pl.ds(s * GROUPS, GROUPS), pl.ds(lo, hi - lo))
        return pltpu.make_async_remote_copy(
            src_ref=edge_out.at[where],
            dst_ref=edge_in.at[where],
            send_sem=edge_send.at[c, s],
            recv_sem=edge_recv.at[c, s],
            device_id=grid_peer(1 if s == 0 else -1),
            device_id_type=MESH,
        )

    y_copy = pltpu.make_async_remote_copy(
        src_ref=y_out,
        dst_ref=y_in,
        send_sem=y_send,
        recv_sem=y_recv,
        device_id={"member": m, "grid": (g + 1 + side * (GRID - 2)) % GRID},
        device_id_type=MESH,
    )

    for c, (lo, hi) in enumerate(CHUNKS):
        x_loads[c].wait()

        def align(n, _):
            for k in range(GROUPS):
                before, left, right, after = aligned(xin[k, n])
                edge_out[k, n] = after
                edge_out[GROUPS + k, n] = before
                parts[k, n] = left
                parts[GROUPS + k, n] = right
            return 0

        lax.fori_loop(lo, hi, align, 0)
        if c == 0:
            pl.semaphore_wait(barrier, len(peers))
        for s in range(2):
            edge_copy(c, s).start()

    y_load.wait()
    w_load.wait()
    full = rows // 8 * 8
    spread = y_rows.shape[0] // tiles

    def turn(t, _):
        cols = pl.ds(pl.multiple_of(t * LANES, LANES), LANES)
        for n in range(0, spread, 8):
            r = pl.multiple_of(jnp.minimum(row0 - group + n, full - 8), 8)
            value = yin[pl.ds(r, 8), cols]
            if n + 8 == spread:
                rest = jnp.zeros((8 + full - rows, LANES), F32)
                tail = jnp.concatenate([yin[pl.ds(full, rows - full), cols], rest], axis=0)
                value = jnp.where(group == GROUPS - 1, tail, value)
            y_rows[pl.ds(n * tiles + t, 8, stride=tiles), :] = value
        return 0

    lax.fori_loop(0, tiles, turn, 0)

    def put_truth(n, row):
        before, left, right, after = aligned(row)
        y_out[n] = jnp.where(side == 0, after, before)
        y_own[n] = jnp.where(side == 0, left, right)

    def align_truth(n, _):
        put_truth(n, y_rows[pl.ds(pl.multiple_of((group + n) * tiles, tiles), tiles), :])
        return 0

    lax.fori_loop(0, share, align_truth, 0)
    put_truth(share, win[...])
    y_copy.start()

    def part_copy(c, p):
        lo, hi = CHUNKS[c]
        peer = member_peer(p)
        return pltpu.make_async_remote_copy(
            src_ref=parts.at[peer["member"], pl.ds(lo, hi - lo)],
            dst_ref=xs.at[m, pl.ds(lo, hi - lo)],
            send_sem=part_send.at[c, p],
            recv_sem=part_recv.at[c, p],
            device_id=peer,
            device_id_type=MESH,
        )

    def own_copy(c):
        lo, hi = CHUNKS[c]
        return pltpu.make_async_copy(
            parts.at[m, pl.ds(lo, hi - lo)], xs.at[m, pl.ds(lo, hi - lo)], own_sem.at[c]
        )

    def owned(s):
        cell = s * edge + sub * LANES + lane
        return (cell >= lo_cell) & (cell < hi_cell)

    in_half = [owned(0), owned(1)]
    for c, (lo, hi) in enumerate(CHUNKS):
        for s in range(2):
            edge_copy(c, s).wait_recv()

        def merge(n, _):
            for k in range(MEMBERS):
                parts[k, n] = jnp.where(in_half[k // GROUPS], parts[k, n], edge_in[k, n])
            return 0

        lax.fori_loop(lo, hi, merge, 0)
        for p in range(1, MEMBERS):
            part_copy(c, p).start()
        own_copy(c).start()

    y_copy.wait_recv()
    in_own = owned(side)

    def merge_truth(n, _):
        y_own[n] = jnp.where(in_own, y_own[n], y_in[n])
        return 0

    lax.fori_loop(0, share + 1, merge_truth, 0)
    own_area = y_own[share]

    def load_row(n):
        x = [xs[k, n] for k in range(MEMBERS)]
        y = y_own[n]
        return x, y, penalty[row0 + n] * own_area

    sums = (jnp.zeros((8, LANES), F32),) * ENTRIES
    for c, (lo, hi) in enumerate(CHUNKS):
        own_copy(c).wait()
        for p in range(1, MEMBERS):
            part_copy(c, p).wait_recv()

        def add(n, sums):
            sums = list(sums)
            x, y, lw = load_row(n)
            for k in range(MEMBERS):
                d = x[k] - y
                sums[k] = sums[k] + lw * d * d
            for e, (a, b) in enumerate(PAIRS):
                d = x[a] - x[b]
                sums[MEMBERS + e] = sums[MEMBERS + e] + lw * d * d
            return tuple(sums)

        sums = lax.fori_loop(lo, hi, add, sums)

    message = jnp.zeros((8, LANES), F32)
    for e in range(0, ENTRIES, 8):
        column = [jnp.sum(s, axis=0, keepdims=True) for s in sums[e : e + 8]]
        column += [jnp.zeros((1, LANES), F32)] * (8 - len(column))
        total = jnp.sum(jnp.concatenate(column, axis=0), axis=1, keepdims=True)
        message = jnp.where(lane == e // 8, total, message)

    def exchange(message, buffer, send, recv, peer_of, count, place):
        buffer[place] = message
        copies = [
            pltpu.make_async_remote_copy(
                src_ref=buffer.at[place],
                dst_ref=buffer.at[place],
                send_sem=send.at[p],
                recv_sem=recv.at[p],
                device_id=peer_of(p),
                device_id_type=MESH,
            )
            for p in range(1, count)
        ]
        for copy in copies:
            copy.start()
        for copy in copies:
            copy.wait_recv()
        total = buffer[0]
        for i in range(1, count):
            total = total + buffer[i]
        return total, copies

    message, first_copies = exchange(
        message, first, first_send, first_recv, first_peer, NX * NY, my * NX + gx
    )
    message, second_copies = exchange(
        message, second, second_send, second_recv, second_peer, NZ * NC, gz * NC + mc
    )

    scale = 1.0 / (rows * half * GRID)
    distance = jnp.sqrt(message * scale + 1e-06)
    entry = lane * 8 + sub
    is_truth = entry < MEMBERS
    share_of = jnp.where(is_truth, 1.0 / MEMBERS, -1.0 / (MEMBERS * (MEMBERS - 1)))
    loss[...] = jnp.sum(jnp.where(entry < ENTRIES, distance * share_of, 0.0), keepdims=True)
    factor = jnp.where(is_truth, 1.0, 1.0 / (MEMBERS - 1)) / distance
    for e in range(ENTRIES):
        coef[e] = jnp.broadcast_to(factor[e % 8 : e % 8 + 1, e // 8 : e // 8 + 1], (8, LANES))

    def place_of(c):
        lo, hi = RETURNS[c]
        return out.at[pl.ds(row0 + lo, hi - lo), pl.ds(pl.multiple_of(side * 8, 8), 8)]

    def res_copy(c, p):
        lo, hi = RETURNS[c]
        peer = member_peer(p)
        return pltpu.make_async_remote_copy(
            src_ref=result.at[peer["member"], pl.ds(lo, hi - lo)],
            dst_ref=place_of(c),
            send_sem=res_send.at[c, p],
            recv_sem=res_recv.at[c, p],
            device_id=peer,
            device_id_type=MESH,
        )

    def keep_copy(c):
        lo, hi = RETURNS[c]
        return pltpu.make_async_copy(
            result.at[m, pl.ds(lo, hi - lo)], place_of(c), keep_sem.at[c]
        )

    for c, (lo, hi) in enumerate(RETURNS):

        def derive(n, _):
            x, y, lw = load_row(n)
            o = [(x[k] - y) * coef[k] for k in range(MEMBERS)]
            for e, (a, b) in enumerate(PAIRS):
                d = (x[a] - x[b]) * coef[MEMBERS + e]
                o[a] = o[a] - d
                o[b] = o[b] + d
            for k in range(MEMBERS):
                result[k, n] = lw * o[k]
            return 0

        lax.fori_loop(lo, hi, derive, 0)
        for p in range(1, MEMBERS):
            res_copy(c, p).start()
        keep_copy(c).start()

    for c in range(chunks):
        for s in range(2):
            edge_copy(c, s).wait_send()
        for p in range(1, MEMBERS):
            part_copy(c, p).wait_send()
    y_copy.wait_send()
    for copy in first_copies + second_copies:
        copy.wait_send()
    for c in range(len(RETURNS)):
        keep_copy(c).wait()
        for p in range(1, MEMBERS):
            res_copy(c, p).wait_send()
            res_copy(c, p).wait_recv()


def local(prediction, reference_state, penalty, area, starts):
    rows, slots = prediction.shape[1:]
    tiles = slots // LANES
    share = rows // GROUPS
    spread = -(-(share + GROUPS - 1) // 8) * 8
    chunks, returns = len(CHUNKS), len(RETURNS)
    vmem = functools.partial(pltpu.VMEM, dtype=F32)
    array = functools.partial(jax.ShapeDtypeStruct, dtype=F32)
    dma = pltpu.SemaphoreType.DMA
    in_smem = pl.BlockSpec(memory_space=pltpu.SMEM)
    anywhere = pl.BlockSpec(memory_space=pl.ANY)
    fields = (MEMBERS, share, 8, LANES)
    y_share = (share + 1, 8, LANES)
    result, loss = pl.pallas_call(
        kernel,
        name="energy_score",
        out_shape=(array((rows, tiles // 2, LANES)), array((1, 1))),
        in_specs=[in_smem, in_smem, anywhere, anywhere, anywhere],
        out_specs=(anywhere, pl.BlockSpec(memory_space=pltpu.VMEM)),
        scratch_shapes=[
            vmem((GROUPS, share, tiles, LANES)),
            vmem((rows, slots)),
            vmem((tiles, LANES)),
            vmem((spread * tiles, LANES)),
            vmem(fields),
            vmem(fields),
            vmem(fields),
            vmem(fields),
            vmem(y_share),
            vmem(y_share),
            vmem(y_share),
            vmem(fields),
            vmem((NX * NY, 8, LANES)),
            vmem((NZ * NC, 8, LANES)),
            vmem((ENTRIES, 8, LANES)),
            dma((chunks + 2,)),
            dma((chunks, 2)),
            dma((chunks, 2)),
            dma,
            dma,
            dma((chunks, MEMBERS)),
            dma((chunks, MEMBERS)),
            dma((chunks,)),
            dma((NX * NY,)),
            dma((NX * NY,)),
            dma((NZ * NC,)),
            dma((NZ * NC,)),
            dma((returns, MEMBERS)),
            dma((returns, MEMBERS)),
            dma((returns,)),
        ],
        compiler_params=pltpu.CompilerParams(
            collective_id=0, has_side_effects=True, vmem_limit_bytes=VMEM_BYTES
        ),
    )(
        starts,
        penalty,
        prediction.reshape(GROUPS, share, tiles, LANES),
        reference_state,
        area.reshape(tiles, LANES),
    )
    return (result.reshape(1, rows, slots // 2), loss.reshape(()))


def solution(mesh):
    placed = (P("member", None, "grid"), P(None, "grid"), P(), P("grid"), P())
    return jax.shard_map(
        local,
        mesh=mesh,
        in_specs=placed,
        out_specs=(P("member", None, "grid"), P()),
        check_vma=False,
    )
```

```python
import functools

import jax
import jax.numpy as jnp
from jax import lax
from jax.experimental import pallas as pl
from jax.experimental.pallas import tpu as pltpu
from jax.sharding import PartitionSpec as P

MESH = pl.DeviceIdType.MESH
F32 = jnp.float32
LANES = 128
VMEM_BYTES = 56 * 2**20
CHUNKS = ((0, 5), (5, 10), (10, 15), (15, 20), (20, 25))
RETURNS = ((0, 3), (3, 12), (12, 25))
NX, NZ = 4, 8
NY, NC = 4, 2
MEMBERS = 8
GRID = 32
GROUPS = MEMBERS // 2
PAIRS = [(a, b) for a in range(MEMBERS) for b in range(a + 1, MEMBERS)]
ENTRIES = MEMBERS + len(PAIRS)


def ring(step, count):
    return min(step, count - step)


FIRST = sorted(range(1, NX * NY), key=lambda p: -ring(p // NX, NY) - ring(p % NX, NX))
SECOND = sorted(range(1, NZ * NC), key=lambda p: (-ring(p // NC, NZ), -(p % NC)))
PEERS = sorted(range(1, MEMBERS), key=lambda p: -ring(p // NC, NY))


def kernel(
    starts,
    penalty,
    pred,
    truth,
    area,
    out,
    loss,
    xin,
    yin,
    win,
    y_rows,
    edge_out,
    edge_in,
    parts,
    xs,
    y_out,
    y_in,
    y_own,
    result,
    first,
    second,
    coef,
    load_sem,
    edge_send,
    edge_recv,
    y_send,
    y_recv,
    part_send,
    part_recv,
    own_sem,
    first_send,
    first_recv,
    second_send,
    second_recv,
    res_send,
    res_recv,
    keep_sem,
):
    share, tiles = pred.shape[1], pred.shape[2]
    rows = share * GROUPS
    edge = tiles // 4 * LANES
    half = 2 * edge
    chunks = len(CHUNKS)
    m = lax.axis_index("member")
    g = lax.axis_index("grid")
    my, mc = m // NC, m % NC
    gx, gz = g // NZ, g % NZ
    side, group = m // GROUPS, m % GROUPS
    row0 = group * share

    def member_peer(p):
        return {"member": (m + p) % MEMBERS, "grid": g}

    def grid_peer(step):
        return {"member": m, "grid": (g + step + GRID) % GRID}

    def first_peer(p):
        return {"member": ((my + p // NX) % NY) * NC + mc, "grid": ((gx + p % NX) % NX) * NZ + gz}

    def second_peer(p):
        return {"member": my * NC + (mc + p % NC) % NC, "grid": gx * NZ + (gz + p // NC) % NZ}

    x_loads = [
        pltpu.make_async_copy(
            pred.at[:, pl.ds(lo, hi - lo)], xin.at[:, pl.ds(lo, hi - lo)], load_sem.at[c]
        )
        for c, (lo, hi) in enumerate(CHUNKS)
    ]
    y_load = pltpu.make_async_copy(truth, yin, load_sem.at[chunks])
    w_load = pltpu.make_async_copy(area, win, load_sem.at[chunks + 1])
    for copy in x_loads + [y_load, w_load]:
        copy.start()

    peers = [member_peer(p) for p in range(1, MEMBERS)]
    peers += [grid_peer(1), grid_peer(-1)]
    peers += [first_peer(p) for p in range(1, NX * NY) if p % NX]
    peers += [second_peer(p) for p in range(NC, NZ * NC)]
    barrier = pltpu.get_barrier_semaphore()
    for peer in peers:
        pl.semaphore_signal(barrier, inc=1, device_id=peer, device_id_type=MESH)

    lo_cell = starts[g] - g * half
    hi_cell = starts[g + 1] - g * half
    shift = lo_cell + edge
    whole = lax.div(shift, LANES)
    part = lax.rem(shift, LANES)
    lane = lax.broadcasted_iota(jnp.int32, (8, LANES), 1)
    wrapped = lax.broadcasted_iota(jnp.int32, (tiles, LANES), 1) >= LANES - part

    def aligned(row):
        now = pltpu.roll(row, whole, 0)
        row = pltpu.roll(jnp.where(wrapped, pltpu.roll(now, 1, 0), now), part, 1)
        return [row[i : i + 8] for i in range(0, tiles, 8)]

    sub = lax.broadcasted_iota(jnp.int32, (8, LANES), 0)

    def edge_copy(c, s):
        lo, hi = CHUNKS[c]
        where = (pl.ds(s * GROUPS, GROUPS), pl.ds(lo, hi - lo))
        return pltpu.make_async_remote_copy(
            src_ref=edge_out.at[where],
            dst_ref=edge_in.at[where],
            send_sem=edge_send.at[c, s],
            recv_sem=edge_recv.at[c, s],
            device_id=grid_peer(1 if s == 0 else -1),
            device_id_type=MESH,
        )

    y_copy = pltpu.make_async_remote_copy(
        src_ref=y_out,
        dst_ref=y_in,
        send_sem=y_send,
        recv_sem=y_recv,
        device_id={"member": m, "grid": (g + 1 + side * (GRID - 2)) % GRID},
        device_id_type=MESH,
    )

    for c, (lo, hi) in enumerate(CHUNKS):
        x_loads[c].wait()

        def align(n, _):
            for k in range(GROUPS):
                before, left, right, after = aligned(xin[k, n])
                edge_out[k, n] = after
                edge_out[GROUPS + k, n] = before
                parts[k, n] = left
                parts[GROUPS + k, n] = right
            return 0

        lax.fori_loop(lo, hi, align, 0)
        if c == 0:
            pl.semaphore_wait(barrier, len(peers))
        for s in range(2):
            edge_copy(c, s).start()

    y_load.wait()
    w_load.wait()
    full = rows // 8 * 8
    spread = y_rows.shape[0] // tiles

    def turn(t, _):
        cols = pl.ds(pl.multiple_of(t * LANES, LANES), LANES)
        for n in range(0, spread, 8):
            r = pl.multiple_of(jnp.minimum(row0 - group + n, full - 8), 8)
            value = yin[pl.ds(r, 8), cols]
            if n + 8 == spread:
                rest = jnp.zeros((8 + full - rows, LANES), F32)
                tail = jnp.concatenate([yin[pl.ds(full, rows - full), cols], rest], axis=0)
                value = jnp.where(group == GROUPS - 1, tail, value)
            y_rows[pl.ds(n * tiles + t, 8, stride=tiles), :] = value
        return 0

    lax.fori_loop(0, tiles, turn, 0)

    def put_truth(n, row):
        before, left, right, after = aligned(row)
        y_out[n] = jnp.where(side == 0, after, before)
        y_own[n] = jnp.where(side == 0, left, right)

    def align_truth(n, _):
        put_truth(n, y_rows[pl.ds(pl.multiple_of((group + n) * tiles, tiles), tiles), :])
        return 0

    lax.fori_loop(0, share, align_truth, 0)
    put_truth(share, win[...])
    y_copy.start()

    def part_copy(c, p):
        lo, hi = CHUNKS[c]
        peer = member_peer(p)
        return pltpu.make_async_remote_copy(
            src_ref=parts.at[peer["member"], pl.ds(lo, hi - lo)],
            dst_ref=xs.at[m, pl.ds(lo, hi - lo)],
            send_sem=part_send.at[c, p],
            recv_sem=part_recv.at[c, p],
            device_id=peer,
            device_id_type=MESH,
        )

    def own_copy(c):
        lo, hi = CHUNKS[c]
        return pltpu.make_async_copy(
            parts.at[m, pl.ds(lo, hi - lo)], xs.at[m, pl.ds(lo, hi - lo)], own_sem.at[c]
        )

    def owned(s):
        cell = s * edge + sub * LANES + lane
        return (cell >= lo_cell) & (cell < hi_cell)

    in_half = [owned(0), owned(1)]
    for c, (lo, hi) in enumerate(CHUNKS):
        for s in range(2):
            edge_copy(c, s).wait_recv()

        def merge(n, _):
            for k in range(MEMBERS):
                parts[k, n] = jnp.where(in_half[k // GROUPS], parts[k, n], edge_in[k, n])
            return 0

        lax.fori_loop(lo, hi, merge, 0)
        for p in PEERS:
            part_copy(c, p).start()
        own_copy(c).start()

    y_copy.wait_recv()
    in_own = owned(side)

    def merge_truth(n, _):
        y_own[n] = jnp.where(in_own, y_own[n], y_in[n])
        return 0

    lax.fori_loop(0, share + 1, merge_truth, 0)
    own_area = y_own[share]

    def load_row(n):
        x = [xs[k, n] for k in range(MEMBERS)]
        y = y_own[n]
        return x, y, penalty[row0 + n] * own_area

    sums = (jnp.zeros((8, LANES), F32),) * ENTRIES
    for c, (lo, hi) in enumerate(CHUNKS):
        own_copy(c).wait()
        for p in range(1, MEMBERS):
            part_copy(c, p).wait_recv()

        def add(n, sums):
            sums = list(sums)
            x, y, lw = load_row(n)
            for k in range(MEMBERS):
                d = x[k] - y
                sums[k] = sums[k] + lw * d * d
            for e, (a, b) in enumerate(PAIRS):
                d = x[a] - x[b]
                sums[MEMBERS + e] = sums[MEMBERS + e] + lw * d * d
            return tuple(sums)

        sums = lax.fori_loop(lo, hi, add, sums)

    message = jnp.zeros((8, LANES), F32)
    for e in range(0, ENTRIES, 8):
        column = [jnp.sum(s, axis=0, keepdims=True) for s in sums[e : e + 8]]
        column += [jnp.zeros((1, LANES), F32)] * (8 - len(column))
        total = jnp.sum(jnp.concatenate(column, axis=0), axis=1, keepdims=True)
        message = jnp.where(lane == e // 8, total, message)

    def exchange(message, buffer, send, recv, peer_of, order, place):
        buffer[place] = message
        copies = [
            pltpu.make_async_remote_copy(
                src_ref=buffer.at[place],
                dst_ref=buffer.at[place],
                send_sem=send.at[p],
                recv_sem=recv.at[p],
                device_id=peer_of(p),
                device_id_type=MESH,
            )
            for p in order
        ]
        for copy in copies:
            copy.start()
        for copy in copies:
            copy.wait_recv()
        total = buffer[0]
        for i in range(1, len(order) + 1):
            total = total + buffer[i]
        return total, copies

    message, first_copies = exchange(
        message, first, first_send, first_recv, first_peer, FIRST, my * NX + gx
    )
    message, second_copies = exchange(
        message, second, second_send, second_recv, second_peer, SECOND, gz * NC + mc
    )

    scale = 1.0 / (rows * half * GRID)
    distance = jnp.sqrt(message * scale + 1e-06)
    entry = lane * 8 + sub
    is_truth = entry < MEMBERS
    share_of = jnp.where(is_truth, 1.0 / MEMBERS, -1.0 / (MEMBERS * (MEMBERS - 1)))
    loss[...] = jnp.sum(jnp.where(entry < ENTRIES, distance * share_of, 0.0), keepdims=True)
    factor = jnp.where(is_truth, 1.0, 1.0 / (MEMBERS - 1)) / distance
    for e in range(ENTRIES):
        coef[e] = jnp.broadcast_to(factor[e % 8 : e % 8 + 1, e // 8 : e // 8 + 1], (8, LANES))

    def place_of(c):
        lo, hi = RETURNS[c]
        return out.at[pl.ds(row0 + lo, hi - lo), pl.ds(pl.multiple_of(side * 8, 8), 8)]

    def res_copy(c, p):
        lo, hi = RETURNS[c]
        peer = member_peer(p)
        return pltpu.make_async_remote_copy(
            src_ref=result.at[peer["member"], pl.ds(lo, hi - lo)],
            dst_ref=place_of(c),
            send_sem=res_send.at[c, p],
            recv_sem=res_recv.at[c, p],
            device_id=peer,
            device_id_type=MESH,
        )

    def keep_copy(c):
        lo, hi = RETURNS[c]
        return pltpu.make_async_copy(
            result.at[m, pl.ds(lo, hi - lo)], place_of(c), keep_sem.at[c]
        )

    for c, (lo, hi) in enumerate(RETURNS):

        def derive(n, _):
            x, y, lw = load_row(n)
            o = [(x[k] - y) * coef[k] for k in range(MEMBERS)]
            for e, (a, b) in enumerate(PAIRS):
                d = (x[a] - x[b]) * coef[MEMBERS + e]
                o[a] = o[a] - d
                o[b] = o[b] + d
            for k in range(MEMBERS):
                result[k, n] = lw * o[k]
            return 0

        lax.fori_loop(lo, hi, derive, 0)
        for p in PEERS:
            res_copy(c, p).start()
        keep_copy(c).start()

    for c in range(chunks):
        for s in range(2):
            edge_copy(c, s).wait_send()
        for p in range(1, MEMBERS):
            part_copy(c, p).wait_send()
    y_copy.wait_send()
    for copy in first_copies + second_copies:
        copy.wait_send()
    for c in range(len(RETURNS)):
        keep_copy(c).wait()
        for p in range(1, MEMBERS):
            res_copy(c, p).wait_send()
            res_copy(c, p).wait_recv()


def local(prediction, reference_state, penalty, area, starts):
    rows, slots = prediction.shape[1:]
    tiles = slots // LANES
    share = rows // GROUPS
    spread = -(-(share + GROUPS - 1) // 8) * 8
    chunks, returns = len(CHUNKS), len(RETURNS)
    vmem = functools.partial(pltpu.VMEM, dtype=F32)
    array = functools.partial(jax.ShapeDtypeStruct, dtype=F32)
    dma = pltpu.SemaphoreType.DMA
    in_smem = pl.BlockSpec(memory_space=pltpu.SMEM)
    anywhere = pl.BlockSpec(memory_space=pl.ANY)
    fields = (MEMBERS, share, 8, LANES)
    y_share = (share + 1, 8, LANES)
    result, loss = pl.pallas_call(
        kernel,
        name="energy_score",
        out_shape=(pltpu.VMEM((rows, tiles // 2, LANES), F32), array((1, 1))),
        in_specs=[in_smem, in_smem, anywhere, anywhere, anywhere],
        out_specs=(anywhere, pl.BlockSpec(memory_space=pltpu.VMEM)),
        scratch_shapes=[
            vmem((GROUPS, share, tiles, LANES)),
            vmem((rows, slots)),
            vmem((tiles, LANES)),
            vmem((spread * tiles, LANES)),
            vmem(fields),
            vmem(fields),
            vmem(fields),
            vmem(fields),
            vmem(y_share),
            vmem(y_share),
            vmem(y_share),
            vmem(fields),
            vmem((NX * NY, 8, LANES)),
            vmem((NZ * NC, 8, LANES)),
            vmem((ENTRIES, 8, LANES)),
            dma((chunks + 2,)),
            dma((chunks, 2)),
            dma((chunks, 2)),
            dma,
            dma,
            dma((chunks, MEMBERS)),
            dma((chunks, MEMBERS)),
            dma((chunks,)),
            dma((NX * NY,)),
            dma((NX * NY,)),
            dma((NZ * NC,)),
            dma((NZ * NC,)),
            dma((returns, MEMBERS)),
            dma((returns, MEMBERS)),
            dma((returns,)),
        ],
        compiler_params=pltpu.CompilerParams(
            collective_id=0, has_side_effects=True, vmem_limit_bytes=VMEM_BYTES
        ),
    )(
        starts,
        penalty,
        prediction.reshape(GROUPS, share, tiles, LANES),
        reference_state,
        area.reshape(tiles, LANES),
    )
    return (result.reshape(1, rows, slots // 2), loss.reshape(()))


def solution(mesh):
    placed = (P("member", None, "grid"), P(None, "grid"), P(), P("grid"), P())
    return jax.shard_map(
        local,
        mesh=mesh,
        in_specs=placed,
        out_specs=(P("member", None, "grid"), P()),
        check_vma=False,
    )
```

```python
import functools

import jax
import jax.numpy as jnp
from jax import lax
from jax.experimental import pallas as pl
from jax.experimental.pallas import tpu as pltpu
from jax.sharding import PartitionSpec as P

MESH = pl.DeviceIdType.MESH
F32 = jnp.float32
LANES = 128
VMEM_BYTES = 56 * 2**20
CHUNKS = 5
RETURNS = 5
NX, NZ = 4, 8
NY, NC = 4, 2
MEMBERS = 8
GRID = 32
GROUPS = MEMBERS // 2
PAIRS = [(a, b) for a in range(MEMBERS) for b in range(a + 1, MEMBERS)]
ENTRIES = MEMBERS + len(PAIRS)


def ring(step, count):
    return min(step, count - step)


MEMBER_STEPS = ((0, 1), (2, 0), (1, 0), (3, 0), (2, 1), (1, 1), (3, 1))
FIRST_STEPS = sorted(
    [(y, x) for y in range(NY) for x in range(NX) if y or x],
    key=lambda s: -ring(s[0], NY) - ring(s[1], NX),
)
SECOND_STEPS = sorted(
    [(z, core) for z in range(NZ) for core in range(NC) if z or core],
    key=lambda s: (-ring(s[0], NZ), -s[1]),
)


def repeat(count, body):
    def step(i, carry):
        body(i)
        return carry

    lax.fori_loop(0, count, step, 0)


def kernel(
    starts_in,
    penalty_in,
    pred,
    truth,
    area,
    out,
    loss_out,
    starts,
    penalty,
    loss,
    xin,
    yin,
    win,
    y_rows,
    edge_out,
    edge_in,
    parts,
    xs,
    y_out,
    y_in,
    y_own,
    result,
    first,
    second,
    coef,
    load_sem,
    edge_send,
    edge_recv,
    y_send,
    y_recv,
    part_send,
    part_recv,
    own_sem,
    first_send,
    first_recv,
    second_send,
    second_recv,
    res_send,
    res_recv,
    keep_sem,
    loss_sem,
):
    share, tiles = pred.shape[1], pred.shape[2]
    rows = share * GROUPS
    edge = tiles // 4 * LANES
    half = 2 * edge
    run = share // CHUNKS
    m = lax.axis_index("member")
    g = lax.axis_index("grid")
    my, mc = m // NC, m % NC
    gx, gz = g // NZ, g % NZ
    side, group = m // GROUPS, m % GROUPS
    row0 = group * share

    def moved(z=0, y=0, x=0, core=0):
        member = ((my + y) % NY) * NC + (mc + core) % NC
        return {"member": member, "grid": ((gx + x) % NX) * NZ + (gz + z) % NZ}

    def member_peer(i):
        y, core = MEMBER_STEPS[i]
        y = (y + mc * (NY - 2 * y)) % NY
        return moved(y=y, core=core)

    def grid_peer(step):
        return {"member": m, "grid": (g + step + GRID) % GRID}

    def first_peer(i):
        y, x = FIRST_STEPS[i]
        return moved(y=y, x=x)

    def second_peer(i):
        z, core = SECOND_STEPS[i]
        return moved(z=z, core=core)

    meet = [(ring(z, NZ), moved(z=z, core=core)) for z, core in SECOND_STEPS if z]
    meet += [(ring(y, NY) + ring(x, NX), moved(y=y, x=x)) for y, x in FIRST_STEPS if x]
    meet += [(ring(y, NY), moved(y=y, core=core)) for y, core in MEMBER_STEPS]
    meet += [(2, grid_peer(1)), (2, grid_peer(-1))]
    barrier = pltpu.get_barrier_semaphore()
    for _, peer in sorted(meet, key=lambda entry: -entry[0]):
        pl.semaphore_signal(barrier, inc=1, device_id=peer, device_id_type=MESH)

    def rows_of(c):
        return pl.ds(c * run, run)

    def x_load(c):
        return pltpu.make_async_copy(
            pred.at[:, rows_of(c)], xin.at[:, rows_of(c)], load_sem.at[c]
        )

    y_load = pltpu.make_async_copy(truth, yin, load_sem.at[CHUNKS])
    w_load = pltpu.make_async_copy(area, win, load_sem.at[CHUNKS + 1])
    starts_load = pltpu.make_async_copy(starts_in, starts, load_sem.at[CHUNKS + 2])
    penalty_load = pltpu.make_async_copy(penalty_in, penalty, load_sem.at[CHUNKS + 3])
    starts_load.start()
    repeat(CHUNKS, lambda c: x_load(c).start())
    for copy in (y_load, w_load, penalty_load):
        copy.start()

    starts_load.wait()
    lo_cell = starts[g] - g * half
    hi_cell = starts[g + 1] - g * half
    shift = lo_cell + edge
    whole = lax.div(shift, LANES)
    part = lax.rem(shift, LANES)
    lane = lax.broadcasted_iota(jnp.int32, (8, LANES), 1)
    wrapped = lax.broadcasted_iota(jnp.int32, (tiles, LANES), 1) >= LANES - part

    def aligned(row):
        now = pltpu.roll(row, whole, 0)
        row = pltpu.roll(jnp.where(wrapped, pltpu.roll(now, 1, 0), now), part, 1)
        return [row[i : i + 8] for i in range(0, tiles, 8)]

    sub = lax.broadcasted_iota(jnp.int32, (8, LANES), 0)

    def edge_copy(c, s):
        where = (pl.ds(s * GROUPS, GROUPS), rows_of(c))
        return pltpu.make_async_remote_copy(
            src_ref=edge_out.at[where],
            dst_ref=edge_in.at[where],
            send_sem=edge_send.at[c, s],
            recv_sem=edge_recv.at[c, s],
            device_id=grid_peer(1 if s == 0 else -1),
            device_id_type=MESH,
        )

    y_copy = pltpu.make_async_remote_copy(
        src_ref=y_out,
        dst_ref=y_in,
        send_sem=y_send,
        recv_sem=y_recv,
        device_id={"member": m, "grid": (g + 1 + side * (GRID - 2)) % GRID},
        device_id_type=MESH,
    )

    def part_copy(c, i):
        peer = member_peer(i)
        return pltpu.make_async_remote_copy(
            src_ref=parts.at[peer["member"], rows_of(c)],
            dst_ref=xs.at[m, rows_of(c)],
            send_sem=part_send.at[c, i],
            recv_sem=part_recv.at[c, i],
            device_id=peer,
            device_id_type=MESH,
        )

    def own_copy(c):
        return pltpu.make_async_copy(
            parts.at[m, rows_of(c)], xs.at[m, rows_of(c)], own_sem.at[c]
        )

    def align(n):
        for k in range(GROUPS):
            before, left, right, after = aligned(xin[k, n])
            edge_out[k, n] = after
            edge_out[GROUPS + k, n] = before
            parts[k, n] = left
            parts[GROUPS + k, n] = right

    def send_edges(c):
        x_load(c).wait()
        repeat(run, lambda n: align(c * run + n))

        @pl.when(c == 0)
        def _():
            pl.semaphore_wait(barrier, len(meet))

        for s in range(2):
            edge_copy(c, s).start()

    repeat(CHUNKS, send_edges)
    y_load.wait()
    w_load.wait()
    full = rows // 8 * 8
    spread = y_rows.shape[0] // tiles

    def turn(t):
        cols = pl.ds(pl.multiple_of(t * LANES, LANES), LANES)
        for n in range(0, spread, 8):
            r = pl.multiple_of(jnp.minimum(row0 - group + n, full - 8), 8)
            value = yin[pl.ds(r, 8), cols]
            if n + 8 == spread:
                rest = jnp.zeros((8 + full - rows, LANES), F32)
                tail = jnp.concatenate([yin[pl.ds(full, rows - full), cols], rest], axis=0)
                value = jnp.where(group == GROUPS - 1, tail, value)
            y_rows[pl.ds(n * tiles + t, 8, stride=tiles), :] = value

    repeat(tiles, turn)

    def put_truth(n, row):
        before, left, right, after = aligned(row)
        y_out[n] = jnp.where(side == 0, after, before)
        y_own[n] = jnp.where(side == 0, left, right)

    def align_truth(n):
        put_truth(n, y_rows[pl.ds(pl.multiple_of((group + n) * tiles, tiles), tiles), :])

    repeat(share, align_truth)
    put_truth(share, win[...])
    y_copy.start()

    def owned(s):
        cell = s * edge + sub * LANES + lane
        return (cell >= lo_cell) & (cell < hi_cell)

    in_half = [owned(0), owned(1)]

    def send_parts(c):
        for s in range(2):
            edge_copy(c, s).wait_recv()

        def merge(n):
            for k in range(MEMBERS):
                parts[k, n] = jnp.where(in_half[k // GROUPS], parts[k, n], edge_in[k, n])

        repeat(run, lambda n: merge(c * run + n))
        for i in range(MEMBERS - 1):
            part_copy(c, i).start()
        own_copy(c).start()

    repeat(CHUNKS, send_parts)
    y_copy.wait_recv()
    in_own = owned(side)

    def merge_truth(n):
        y_own[n] = jnp.where(in_own, y_own[n], y_in[n])

    repeat(share + 1, merge_truth)
    own_area = y_own[share]

    def load_row(n):
        x = [xs[k, n] for k in range(MEMBERS)]
        y = y_own[n]
        return x, y, penalty[row0 + n] * own_area

    penalty_load.wait()

    def add(n, sums):
        sums = list(sums)
        x, y, lw = load_row(n)
        for k in range(MEMBERS):
            d = x[k] - y
            sums[k] = sums[k] + lw * d * d
        for e, (a, b) in enumerate(PAIRS):
            d = x[a] - x[b]
            sums[MEMBERS + e] = sums[MEMBERS + e] + lw * d * d
        return tuple(sums)

    def add_run(c, sums):
        own_copy(c).wait()
        for i in range(MEMBERS - 1):
            part_copy(c, i).wait_recv()
        return lax.fori_loop(c * run, c * run + run, add, sums)

    sums = lax.fori_loop(0, CHUNKS, add_run, (jnp.zeros((8, LANES), F32),) * ENTRIES)

    message = jnp.zeros((8, LANES), F32)
    for e in range(0, ENTRIES, 8):
        column = [jnp.sum(s, axis=0, keepdims=True) for s in sums[e : e + 8]]
        column += [jnp.zeros((1, LANES), F32)] * (8 - len(column))
        total = jnp.sum(jnp.concatenate(column, axis=0), axis=1, keepdims=True)
        message = jnp.where(lane == e // 8, total, message)

    def exchange(message, buffer, send, recv, peer_of, place):
        count = buffer.shape[0]
        buffer[place] = message

        def copy(i):
            return pltpu.make_async_remote_copy(
                src_ref=buffer.at[place],
                dst_ref=buffer.at[place],
                send_sem=send.at[i],
                recv_sem=recv.at[i],
                device_id=peer_of(i),
                device_id_type=MESH,
            )

        for i in range(count - 1):
            copy(i).start()
        for i in range(count - 1):
            copy(i).wait_recv()
        total = buffer[0]
        for i in range(1, count):
            total = total + buffer[i]
        return total, copy

    message, first_copy = exchange(
        message, first, first_send, first_recv, first_peer, my * NX + gx
    )
    message, second_copy = exchange(
        message, second, second_send, second_recv, second_peer, gz * NC + mc
    )

    scale = 1.0 / (rows * half * GRID)
    distance = jnp.sqrt(message * scale + 1e-06)
    entry = lane * 8 + sub
    is_truth = entry < MEMBERS
    share_of = jnp.where(is_truth, 1.0 / MEMBERS, -1.0 / (MEMBERS * (MEMBERS - 1)))
    loss[...] = jnp.sum(jnp.where(entry < ENTRIES, distance * share_of, 0.0), keepdims=True)
    loss_copy = pltpu.make_async_copy(loss, loss_out, loss_sem)
    loss_copy.start()
    factor = jnp.where(is_truth, 1.0, 1.0 / (MEMBERS - 1)) / distance
    for e in range(ENTRIES):
        coef[e] = jnp.broadcast_to(factor[e % 8 : e % 8 + 1, e // 8 : e // 8 + 1], (8, LANES))

    back = share // RETURNS

    def back_rows(c):
        return pl.ds(c * back, back)

    def place_of(c):
        return out.at[pl.ds(row0 + c * back, back), pl.ds(pl.multiple_of(side * 8, 8), 8)]

    def res_copy(c, i):
        peer = member_peer(i)
        return pltpu.make_async_remote_copy(
            src_ref=result.at[peer["member"], back_rows(c)],
            dst_ref=place_of(c),
            send_sem=res_send.at[c, i],
            recv_sem=res_recv.at[c, i],
            device_id=peer,
            device_id_type=MESH,
        )

    def keep_copy(c):
        return pltpu.make_async_copy(result.at[m, back_rows(c)], place_of(c), keep_sem.at[c])

    def derive(n):
        x, y, lw = load_row(n)
        o = [(x[k] - y) * coef[k] for k in range(MEMBERS)]
        for e, (a, b) in enumerate(PAIRS):
            d = (x[a] - x[b]) * coef[MEMBERS + e]
            o[a] = o[a] - d
            o[b] = o[b] + d
        for k in range(MEMBERS):
            result[k, n] = lw * o[k]

    def send_back(c):
        repeat(back, lambda n: derive(c * back + n))
        for i in range(MEMBERS - 1):
            res_copy(c, i).start()
        keep_copy(c).start()

    repeat(RETURNS, send_back)

    def end_run(c):
        for s in range(2):
            edge_copy(c, s).wait_send()
        for i in range(MEMBERS - 1):
            part_copy(c, i).wait_send()

    repeat(CHUNKS, end_run)
    y_copy.wait_send()
    for i in range(NX * NY - 1):
        first_copy(i).wait_send()
    for i in range(NZ * NC - 1):
        second_copy(i).wait_send()
    loss_copy.wait()

    def end_back(c):
        keep_copy(c).wait()

        for i in range(MEMBERS - 1):
            res_copy(c, i).wait_send()
            res_copy(c, i).wait_recv()

    repeat(RETURNS, end_back)


def local(prediction, reference_state, penalty, area, starts):
    rows, slots = prediction.shape[1:]
    tiles = slots // LANES
    share = rows // GROUPS
    spread = -(-(share + GROUPS - 1) // 8) * 8
    vmem = functools.partial(pltpu.VMEM, dtype=F32)
    array = functools.partial(jax.ShapeDtypeStruct, dtype=F32)
    dma = pltpu.SemaphoreType.DMA
    anywhere = pl.BlockSpec(memory_space=pl.ANY)
    fields = (MEMBERS, share, 8, LANES)
    y_share = (share + 1, 8, LANES)
    result, loss = pl.pallas_call(
        kernel,
        name="energy_score",
        out_shape=(pltpu.VMEM((rows, tiles // 2, LANES), F32), array((1, 1))),
        in_specs=[anywhere] * 5,
        out_specs=(anywhere, anywhere),
        scratch_shapes=[
            pltpu.SMEM(starts.shape, jnp.int32),
            pltpu.SMEM(penalty.shape, F32),
            vmem((1, 1)),
            vmem((GROUPS, share, tiles, LANES)),
            vmem((rows, slots)),
            vmem((tiles, LANES)),
            vmem((spread * tiles, LANES)),
            vmem(fields),
            vmem(fields),
            vmem(fields),
            vmem(fields),
            vmem(y_share),
            vmem(y_share),
            vmem(y_share),
            vmem(fields),
            vmem((NX * NY, 8, LANES)),
            vmem((NZ * NC, 8, LANES)),
            vmem((ENTRIES, 8, LANES)),
            dma((CHUNKS + 4,)),
            dma((CHUNKS, 2)),
            dma((CHUNKS, 2)),
            dma,
            dma,
            dma((CHUNKS, MEMBERS - 1)),
            dma((CHUNKS, MEMBERS - 1)),
            dma((CHUNKS,)),
            dma((NX * NY - 1,)),
            dma((NX * NY - 1,)),
            dma((NZ * NC - 1,)),
            dma((NZ * NC - 1,)),
            dma((RETURNS, MEMBERS - 1)),
            dma((RETURNS, MEMBERS - 1)),
            dma((RETURNS,)),
            dma,
        ],
        compiler_params=pltpu.CompilerParams(
            collective_id=0, has_side_effects=True, vmem_limit_bytes=VMEM_BYTES
        ),
    )(
        starts,
        penalty,
        prediction.reshape(GROUPS, share, tiles, LANES),
        reference_state,
        area.reshape(tiles, LANES),
    )
    return (result.reshape(1, rows, slots // 2), loss.reshape(()))


def solution(mesh):
    placed = (P("member", None, "grid"), P(None, "grid"), P(), P("grid"), P())
    return jax.shard_map(
        local,
        mesh=mesh,
        in_specs=placed,
        out_specs=(P("member", None, "grid"), P()),
        check_vma=False,
    )
```

```python
import functools

import jax
import jax.numpy as jnp
from jax import lax
from jax.experimental import pallas as pl
from jax.experimental.pallas import tpu as pltpu
from jax.sharding import PartitionSpec as P

MESH = pl.DeviceIdType.MESH
F32 = jnp.float32
LANES = 128
VMEM_BYTES = 56 * 2**20
CHUNKS = ((0, 5), (5, 10), (10, 15), (15, 20), (20, 25))
RETURNS = 5
NX, NZ = 4, 8
NY, NC = 4, 2
MEMBERS = 8
GRID = 32
SIDES = 2
GROUPS = MEMBERS // SIDES
PAIRS = [(a, b) for a in range(MEMBERS) for b in range(a + 1, MEMBERS)]
ENTRIES = MEMBERS + len(PAIRS)


def ring(step, count):
    return min(step, count - step)


MEMBER_STEPS = ((0, 1), (2, 0), (1, 0), (3, 0), (2, 1), (1, 1), (3, 1))
FIRST_STEPS = sorted(
    [(y, x) for y in range(NY) for x in range(NX) if y or x],
    key=lambda s: -ring(s[0], NY) - ring(s[1], NX),
)
SECOND_STEPS = sorted(
    [(z, core) for z in range(NZ) for core in range(NC) if z or core],
    key=lambda s: (-ring(s[0], NZ), -s[1]),
)


def repeat(first, end, body):
    def step(i, carry):
        body(i)
        return carry

    lax.fori_loop(first, end, step, 0)


def wait_for(ref, sem):
    pltpu.make_async_copy(ref, ref, sem).wait()


def kernel(
    starts_in,
    penalty_in,
    pred,
    truth,
    area,
    out,
    loss_out,
    starts,
    penalty,
    loss,
    xin,
    yin,
    win,
    y_rows,
    edge_out,
    edge_in,
    parts,
    xs,
    y_out,
    y_in,
    y_own,
    result,
    first,
    second,
    coef,
    load_sem,
    edge_send,
    edge_recv,
    y_send,
    y_recv,
    part_send,
    part_recv,
    first_send,
    first_recv,
    second_send,
    second_recv,
    res_send,
    res_recv,
    loss_sem,
):
    share, tiles = pred.shape[1], pred.shape[2]
    rows = share * GROUPS
    edge = tiles // 4 * LANES
    half = 2 * edge
    m = lax.axis_index("member")
    g = lax.axis_index("grid")
    my, mc = m // NC, m % NC
    gx, gz = g // NZ, g % NZ
    side, group = m % SIDES, m // SIDES
    row0 = group * share

    def moved(z=0, y=0, x=0, core=0):
        member = ((my + y) % NY) * NC + (mc + core) % NC
        return {"member": member, "grid": ((gx + x) % NX) * NZ + (gz + z) % NZ}

    def member_peer(i):
        y, core = MEMBER_STEPS[i]
        y = (y + mc * (NY - 2 * y)) % NY
        return moved(y=y, core=core)

    def grid_peer(step):
        return {"member": m, "grid": (g + step + GRID) % GRID}

    def first_peer(i):
        y, x = FIRST_STEPS[i]
        return moved(y=y, x=x)

    def second_peer(i):
        z, core = SECOND_STEPS[i]
        return moved(z=z, core=core)

    meet = [(ring(z, NZ), moved(z=z, core=core)) for z, core in SECOND_STEPS if z]
    meet += [(ring(y, NY) + ring(x, NX), moved(y=y, x=x)) for y, x in FIRST_STEPS if x]
    meet += [(ring(y, NY), moved(y=y, core=core)) for y, core in MEMBER_STEPS]
    meet += [(2, grid_peer(1)), (2, grid_peer(-1))]
    barrier = pltpu.get_barrier_semaphore()
    for _, peer in sorted(meet, key=lambda entry: -entry[0]):
        pl.semaphore_signal(barrier, inc=1, device_id=peer, device_id_type=MESH)

    def rows_of(c):
        lo, hi = CHUNKS[c]
        return pl.ds(lo, hi - lo)

    def x_load(c):
        return pltpu.make_async_copy(
            pred.at[:, rows_of(c)], xin.at[:, rows_of(c)], load_sem.at[c]
        )

    y_load = pltpu.make_async_copy(truth, yin, load_sem.at[len(CHUNKS)])
    w_load = pltpu.make_async_copy(area, win, load_sem.at[len(CHUNKS) + 1])
    starts_load = pltpu.make_async_copy(starts_in, starts, load_sem.at[len(CHUNKS) + 2])
    penalty_load = pltpu.make_async_copy(penalty_in, penalty, load_sem.at[len(CHUNKS) + 3])
    starts_load.start()
    for c in range(len(CHUNKS)):
        x_load(c).start()
    for copy in (y_load, w_load, penalty_load):
        copy.start()

    starts_load.wait()
    lo_cell = starts[g] - g * half
    hi_cell = starts[g + 1] - g * half
    shift = lo_cell + edge
    whole = lax.div(shift, LANES)
    part = lax.rem(shift, LANES)
    lane = lax.broadcasted_iota(jnp.int32, (8, LANES), 1)
    wrapped = lax.broadcasted_iota(jnp.int32, (tiles, LANES), 1) >= LANES - part

    def aligned(row):
        now = pltpu.roll(row, whole, 0)
        row = pltpu.roll(jnp.where(wrapped, pltpu.roll(now, 1, 0), now), part, 1)
        return [row[i : i + 8] for i in range(0, tiles, 8)]

    sub = lax.broadcasted_iota(jnp.int32, (8, LANES), 0)

    def edge_copy(c, s):
        where = (s, slice(None), rows_of(c))
        return pltpu.make_async_remote_copy(
            src_ref=edge_out.at[where],
            dst_ref=edge_in.at[where],
            send_sem=edge_send,
            recv_sem=edge_recv.at[c],
            device_id=grid_peer(1 if s == 0 else -1),
            device_id_type=MESH,
        )

    y_copy = pltpu.make_async_remote_copy(
        src_ref=y_out,
        dst_ref=y_in,
        send_sem=y_send,
        recv_sem=y_recv,
        device_id={"member": m, "grid": (g + 1 + side * (GRID - 2)) % GRID},
        device_id_type=MESH,
    )

    def part_copy(c, i):
        peer = member_peer(i)
        return pltpu.make_async_remote_copy(
            src_ref=parts.at[peer["member"], rows_of(c)],
            dst_ref=xs.at[m, rows_of(c)],
            send_sem=part_send,
            recv_sem=part_recv.at[c],
            device_id=peer,
            device_id_type=MESH,
        )

    def own_copy(c):
        return pltpu.make_async_copy(
            parts.at[m, rows_of(c)], xs.at[m, rows_of(c)], part_recv.at[c]
        )

    def send_parts(c):
        for i in range(MEMBERS - 1):
            part_copy(c, i).start()
        own_copy(c).start()

    def align(n):
        for k in range(GROUPS):
            before, left, right, after = aligned(xin[k, n])
            edge_out[0, k, n] = after
            edge_out[1, k, n] = before
            parts[SIDES * k, n] = left
            parts[SIDES * k + 1, n] = right

    for c, (lo, hi) in enumerate(CHUNKS):
        x_load(c).wait()
        repeat(lo, hi, align)
        if c == 0:
            pl.semaphore_wait(barrier, len(meet))
        for s in range(SIDES):
            edge_copy(c, s).start()

    y_load.wait()
    w_load.wait()
    full = rows // 8 * 8
    spread = y_rows.shape[0] // tiles

    def turn(t):
        cols = pl.ds(pl.multiple_of(t * LANES, LANES), LANES)
        for n in range(0, spread, 8):
            r = pl.multiple_of(jnp.minimum(row0 - group + n, full - 8), 8)
            value = yin[pl.ds(r, 8), cols]
            if n + 8 == spread:
                rest = jnp.zeros((8 + full - rows, LANES), F32)
                tail = jnp.concatenate([yin[pl.ds(full, rows - full), cols], rest], axis=0)
                value = jnp.where(group == GROUPS - 1, tail, value)
            y_rows[pl.ds(n * tiles + t, 8, stride=tiles), :] = value

    repeat(0, tiles, turn)

    def put_truth(n, row):
        before, left, right, after = aligned(row)
        y_out[n] = jnp.where(side == 0, after, before)
        y_own[n] = jnp.where(side == 0, left, right)

    def align_truth(n):
        put_truth(n, y_rows[pl.ds(pl.multiple_of((group + n) * tiles, tiles), tiles), :])

    repeat(0, share, align_truth)
    put_truth(share, win[...])
    y_copy.start()

    def owned(s):
        cell = s * edge + sub * LANES + lane
        return (cell >= lo_cell) & (cell < hi_cell)

    in_half = [owned(0), owned(1)]

    def merge(n):
        for k in range(MEMBERS):
            s = k % SIDES
            parts[k, n] = jnp.where(in_half[s], parts[k, n], edge_in[s, k // SIDES, n])

    for c, (lo, hi) in enumerate(CHUNKS):
        wait_for(edge_in.at[:, :, rows_of(c)], edge_recv.at[c])
        repeat(lo, hi, merge)
        send_parts(c)

    y_copy.wait_recv()
    in_own = owned(side)

    def merge_truth(n):
        y_own[n] = jnp.where(in_own, y_own[n], y_in[n])

    repeat(0, share + 1, merge_truth)
    own_area = y_own[share]

    def load_row(n):
        x = [xs[k, n] for k in range(MEMBERS)]
        y = y_own[n]
        return x, y, penalty[row0 + n] * own_area

    penalty_load.wait()

    def add(n, sums):
        sums = list(sums)
        x, y, lw = load_row(n)
        for k in range(MEMBERS):
            d = x[k] - y
            sums[k] = sums[k] + lw * d * d
        for e, (a, b) in enumerate(PAIRS):
            d = x[a] - x[b]
            sums[MEMBERS + e] = sums[MEMBERS + e] + lw * d * d
        return tuple(sums)

    sums = (jnp.zeros((8, LANES), F32),) * ENTRIES
    for c, (lo, hi) in enumerate(CHUNKS):
        wait_for(xs.at[:, rows_of(c)], part_recv.at[c])
        sums = lax.fori_loop(lo, hi, add, sums)

    message = jnp.zeros((8, LANES), F32)
    for e in range(0, ENTRIES, 8):
        column = [jnp.sum(s, axis=0, keepdims=True) for s in sums[e : e + 8]]
        column += [jnp.zeros((1, LANES), F32)] * (8 - len(column))
        total = jnp.sum(jnp.concatenate(column, axis=0), axis=1, keepdims=True)
        message = jnp.where(lane == e // 8, total, message)

    def exchange(message, buffer, send, recv, peer_of, place):
        count = buffer.shape[0]
        buffer[place] = message

        for i in range(count - 1):
            pltpu.make_async_remote_copy(
                src_ref=buffer.at[place],
                dst_ref=buffer.at[place],
                send_sem=send,
                recv_sem=recv,
                device_id=peer_of(i),
                device_id_type=MESH,
            ).start()
        wait_for(buffer.at[pl.ds(0, count - 1)], recv)
        total = buffer[0]
        for i in range(1, count):
            total = total + buffer[i]
        return total

    message = exchange(
        message, first, first_send, first_recv, first_peer, my * NX + gx
    )
    message = exchange(
        message, second, second_send, second_recv, second_peer, gz * NC + mc
    )

    scale = 1.0 / (rows * half * GRID)
    distance = jnp.sqrt(message * scale + 1e-06)
    entry = lane * 8 + sub
    is_truth = entry < MEMBERS
    share_of = jnp.where(is_truth, 1.0 / MEMBERS, -1.0 / (MEMBERS * (MEMBERS - 1)))
    loss[...] = jnp.sum(jnp.where(entry < ENTRIES, distance * share_of, 0.0), keepdims=True)
    loss_copy = pltpu.make_async_copy(loss, loss_out, loss_sem)
    loss_copy.start()
    factor = jnp.where(is_truth, 1.0, 1.0 / (MEMBERS - 1)) / distance
    for e in range(ENTRIES):
        coef[e] = jnp.broadcast_to(factor[e % 8 : e % 8 + 1, e // 8 : e // 8 + 1], (8, LANES))

    back = share // RETURNS

    def back_rows(c):
        return pl.ds(c * back, back)

    def place_of(c):
        return out.at[pl.ds(row0 + c * back, back), pl.ds(pl.multiple_of(side * 8, 8), 8)]

    def res_copy(c, i):
        peer = member_peer(i)
        return pltpu.make_async_remote_copy(
            src_ref=result.at[peer["member"], back_rows(c)],
            dst_ref=place_of(c),
            send_sem=res_send,
            recv_sem=res_recv,
            device_id=peer,
            device_id_type=MESH,
        )

    def keep_copy(c):
        return pltpu.make_async_copy(result.at[m, back_rows(c)], place_of(c), res_recv)

    def derive(n):
        x, y, lw = load_row(n)
        o = [(x[k] - y) * coef[k] for k in range(MEMBERS)]
        for e, (a, b) in enumerate(PAIRS):
            d = (x[a] - x[b]) * coef[MEMBERS + e]
            o[a] = o[a] - d
            o[b] = o[b] + d
        for k in range(MEMBERS):
            result[k, n] = lw * o[k]

    def send_back(c):
        repeat(c * back, c * back + back, derive)
        for i in range(MEMBERS - 1):
            res_copy(c, i).start()
        keep_copy(c).start()

    repeat(0, RETURNS, send_back)

    wait_for(edge_out, edge_send)
    wait_for(parts.at[pl.ds(0, MEMBERS - 1)], part_send)
    y_copy.wait_send()
    wait_for(first.at[pl.ds(0, NX * NY - 1)], first_send)
    wait_for(second.at[pl.ds(0, NZ * NC - 1)], second_send)
    loss_copy.wait()
    wait_for(result.at[pl.ds(0, MEMBERS - 1)], res_send)
    wait_for(out, res_recv)


def local(prediction, reference_state, penalty, area, starts):
    rows, slots = prediction.shape[1:]
    tiles = slots // LANES
    share = rows // GROUPS
    spread = -(-(share + GROUPS - 1) // 8) * 8
    vmem = functools.partial(pltpu.VMEM, dtype=F32)
    array = functools.partial(jax.ShapeDtypeStruct, dtype=F32)
    dma = pltpu.SemaphoreType.DMA
    anywhere = pl.BlockSpec(memory_space=pl.ANY)
    fields = (MEMBERS, share, 8, LANES)
    edges = (SIDES, GROUPS, share, 8, LANES)
    runs = len(CHUNKS)
    y_share = (share + 1, 8, LANES)
    result, loss = pl.pallas_call(
        kernel,
        name="energy_score",
        out_shape=(pltpu.VMEM((rows, tiles // 2, LANES), F32), array((1, 1))),
        in_specs=[anywhere] * 5,
        out_specs=(anywhere, anywhere),
        scratch_shapes=[
            pltpu.SMEM(starts.shape, jnp.int32),
            pltpu.SMEM(penalty.shape, F32),
            vmem((1, 1)),
            vmem((GROUPS, share, tiles, LANES)),
            vmem((rows, slots)),
            vmem((tiles, LANES)),
            vmem((spread * tiles, LANES)),
            vmem(edges),
            vmem(edges),
            vmem(fields),
            vmem(fields),
            vmem(y_share),
            vmem(y_share),
            vmem(y_share),
            vmem(fields),
            vmem((NX * NY, 8, LANES)),
            vmem((NZ * NC, 8, LANES)),
            vmem((ENTRIES, 8, LANES)),
            dma((runs + 4,)),
            dma,
            dma((runs,)),
            dma,
            dma,
            dma,
            dma((runs,)),
            dma,
            dma,
            dma,
            dma,
            dma,
            dma,
            dma,
        ],
        compiler_params=pltpu.CompilerParams(
            collective_id=0, has_side_effects=True, vmem_limit_bytes=VMEM_BYTES
        ),
    )(
        starts,
        penalty,
        prediction.reshape(GROUPS, share, tiles, LANES),
        reference_state,
        area.reshape(tiles, LANES),
    )
    return (result.reshape(1, rows, slots // 2), loss.reshape(()))


def solution(mesh):
    placed = (P("member", None, "grid"), P(None, "grid"), P(), P("grid"), P())
    return jax.shard_map(
        local,
        mesh=mesh,
        in_specs=placed,
        out_specs=(P("member", None, "grid"), P()),
        check_vma=False,
    )
```

```python
import functools
import itertools
import math

import jax
import jax.numpy as jnp
from jax import lax
from jax.experimental import pallas as pl
from jax.experimental.pallas import tpu as pltpu
from jax.sharding import PartitionSpec as P

MESH = pl.DeviceIdType.MESH
F32 = jnp.float32
LANES = 128
VMEM_BYTES = 56 * 2**20
CHUNKS = ((0, 3), (3, 7), (7, 11), (11, 15), (15, 19), (19, 22), (22, 25))
RETURNS = 5
NX, NZ = 4, 8
NY, NC = 4, 2
MEMBERS = 8
GRID = 32
SIDES = 2
GROUPS = MEMBERS // SIDES
PAIRS = [(a, b) for a in range(MEMBERS) for b in range(a + 1, MEMBERS)]
ENTRIES = MEMBERS + len(PAIRS)


AXES = {"z": NZ, "y": NY, "x": NX, "core": NC}
STAGES = (("z", "core"), ("y", "x"))


def hops(step):
    return sum(min(step[a], AXES[a] - step[a]) for a in step)


def steps(axes):
    ways = itertools.product(*(range(AXES[a]) for a in axes))
    ways = [dict(zip(axes, way)) for way in ways if any(way)]
    return sorted(ways, key=lambda way: -hops(way))


MEMBER_STEPS = ((0, 1), (2, 0), (1, 0), (3, 0), (2, 1), (1, 1), (3, 1))
MEET = [dict(y=y, core=core) for y, core in MEMBER_STEPS]
for axes in STAGES:
    MEET += [way for way in steps(axes) if set(k for k in way if way[k]) - {"y", "core"}]


def repeat(first, end, body):
    def step(i, carry):
        body(i)
        return carry

    lax.fori_loop(first, end, step, 0)


def wait_for(ref, sem):
    pltpu.make_async_copy(ref, ref, sem).wait()


def kernel(
    starts_in,
    penalty_in,
    pred,
    truth,
    area,
    out,
    loss_out,
    starts,
    penalty,
    loss,
    xin,
    yin,
    win,
    y_rows,
    edge_out,
    edge_in,
    parts,
    xs,
    y_out,
    y_in,
    y_own,
    result,
    first,
    second,
    coef,
    load_sem,
    edge_send,
    edge_recv,
    y_send,
    y_recv,
    part_send,
    part_recv,
    first_send,
    first_recv,
    second_send,
    second_recv,
    res_send,
    res_recv,
    loss_sem,
):
    share, tiles = pred.shape[1], pred.shape[2]
    rows = share * GROUPS
    edge = tiles // 4 * LANES
    half = 2 * edge
    m = lax.axis_index("member")
    g = lax.axis_index("grid")
    my, mc = m // NC, m % NC
    gx, gz = g // NZ, g % NZ
    side, group = m % SIDES, m // SIDES
    row0 = group * share

    def moved(z=0, y=0, x=0, core=0):
        member = ((my + y) % NY) * NC + (mc + core) % NC
        return {"member": member, "grid": ((gx + x) % NX) * NZ + (gz + z) % NZ}

    def member_peer(i):
        y, core = MEMBER_STEPS[i]
        y = (y + mc * (NY - 2 * y)) % NY
        return moved(y=y, core=core)

    def grid_peer(step):
        return {"member": m, "grid": (g + step + GRID) % GRID}

    here = {"z": gz, "y": my, "x": gx, "core": mc}
    meet = [(hops(way), moved(**way)) for way in MEET]
    meet += [(2, grid_peer(1)), (2, grid_peer(-1))]
    barrier = pltpu.get_barrier_semaphore()
    for _, peer in sorted(meet, key=lambda entry: -entry[0]):
        pl.semaphore_signal(barrier, inc=1, device_id=peer, device_id_type=MESH)

    def rows_of(c):
        lo, hi = CHUNKS[c]
        return pl.ds(lo, hi - lo)

    def x_load(c):
        return pltpu.make_async_copy(
            pred.at[:, rows_of(c)], xin.at[:, rows_of(c)], load_sem.at[c]
        )

    y_load = pltpu.make_async_copy(truth, yin, load_sem.at[len(CHUNKS)])
    w_load = pltpu.make_async_copy(area, win, load_sem.at[len(CHUNKS) + 1])
    starts_load = pltpu.make_async_copy(starts_in, starts, load_sem.at[len(CHUNKS) + 2])
    penalty_load = pltpu.make_async_copy(penalty_in, penalty, load_sem.at[len(CHUNKS) + 3])
    starts_load.start()
    for c in range(len(CHUNKS)):
        x_load(c).start()
    for copy in (y_load, w_load, penalty_load):
        copy.start()

    starts_load.wait()
    lo_cell = starts[g] - g * half
    hi_cell = starts[g + 1] - g * half
    shift = lo_cell + edge
    whole = lax.div(shift, LANES)
    part = lax.rem(shift, LANES)
    lane = lax.broadcasted_iota(jnp.int32, (8, LANES), 1)
    wrapped = lax.broadcasted_iota(jnp.int32, (tiles, LANES), 1) >= LANES - part

    def aligned(row):
        now = pltpu.roll(row, whole, 0)
        row = pltpu.roll(jnp.where(wrapped, pltpu.roll(now, 1, 0), now), part, 1)
        return [row[i : i + 8] for i in range(0, tiles, 8)]

    sub = lax.broadcasted_iota(jnp.int32, (8, LANES), 0)

    def edge_copy(c, s):
        where = (s, slice(None), rows_of(c))
        return pltpu.make_async_remote_copy(
            src_ref=edge_out.at[where],
            dst_ref=edge_in.at[where],
            send_sem=edge_send,
            recv_sem=edge_recv.at[c],
            device_id=grid_peer(1 if s == 0 else -1),
            device_id_type=MESH,
        )

    y_copy = pltpu.make_async_remote_copy(
        src_ref=y_out,
        dst_ref=y_in,
        send_sem=y_send,
        recv_sem=y_recv,
        device_id={"member": m, "grid": (g + 1 + side * (GRID - 2)) % GRID},
        device_id_type=MESH,
    )

    def part_copy(c, i):
        peer = member_peer(i)
        return pltpu.make_async_remote_copy(
            src_ref=parts.at[peer["member"], rows_of(c)],
            dst_ref=xs.at[m, rows_of(c)],
            send_sem=part_send,
            recv_sem=part_recv.at[c],
            device_id=peer,
            device_id_type=MESH,
        )

    def own_copy(c):
        return pltpu.make_async_copy(
            parts.at[m, rows_of(c)], xs.at[m, rows_of(c)], part_recv.at[c]
        )

    def send_parts(c):
        for i in range(MEMBERS - 1):
            part_copy(c, i).start()
        own_copy(c).start()

    def align(n):
        for k in range(GROUPS):
            before, left, right, after = aligned(xin[k, n])
            edge_out[0, k, n] = after
            edge_out[1, k, n] = before
            parts[SIDES * k, n] = left
            parts[SIDES * k + 1, n] = right

    for c, (lo, hi) in enumerate(CHUNKS):
        x_load(c).wait()
        repeat(lo, hi, align)
        if c == 0:
            pl.semaphore_wait(barrier, len(meet))
        for s in range(SIDES):
            edge_copy(c, s).start()

    y_load.wait()
    w_load.wait()
    full = rows // 8 * 8
    spread = y_rows.shape[0] // tiles

    def turn(t):
        cols = pl.ds(pl.multiple_of(t * LANES, LANES), LANES)
        for n in range(0, spread, 8):
            r = pl.multiple_of(jnp.minimum(row0 - group + n, full - 8), 8)
            value = yin[pl.ds(r, 8), cols]
            if n + 8 == spread:
                rest = jnp.zeros((8 + full - rows, LANES), F32)
                tail = jnp.concatenate([yin[pl.ds(full, rows - full), cols], rest], axis=0)
                value = jnp.where(group == GROUPS - 1, tail, value)
            y_rows[pl.ds(n * tiles + t, 8, stride=tiles), :] = value

    repeat(0, tiles, turn)

    def put_truth(n, row):
        before, left, right, after = aligned(row)
        y_out[n] = jnp.where(side == 0, after, before)
        y_own[n] = jnp.where(side == 0, left, right)

    def align_truth(n):
        put_truth(n, y_rows[pl.ds(pl.multiple_of((group + n) * tiles, tiles), tiles), :])

    repeat(0, share, align_truth)
    put_truth(share, win[...])
    y_copy.start()

    def owned(s):
        cell = s * edge + sub * LANES + lane
        return (cell >= lo_cell) & (cell < hi_cell)

    in_half = [owned(0), owned(1)]

    def merge(n):
        for k in range(MEMBERS):
            s = k % SIDES
            parts[k, n] = jnp.where(in_half[s], parts[k, n], edge_in[s, k // SIDES, n])

    for c, (lo, hi) in enumerate(CHUNKS):
        wait_for(edge_in.at[:, :, rows_of(c)], edge_recv.at[c])
        repeat(lo, hi, merge)
        send_parts(c)

    y_copy.wait_recv()
    in_own = owned(side)

    def merge_truth(n):
        y_own[n] = jnp.where(in_own, y_own[n], y_in[n])

    repeat(0, share + 1, merge_truth)
    own_area = y_own[share]

    def load_row(n):
        x = [xs[k, n] for k in range(MEMBERS)]
        y = y_own[n]
        return x, y, penalty[row0 + n] * own_area

    penalty_load.wait()

    def add(n, sums):
        sums = list(sums)
        x, y, lw = load_row(n)
        for k in range(MEMBERS):
            d = x[k] - y
            sums[k] = sums[k] + lw * d * d
        for e, (a, b) in enumerate(PAIRS):
            d = x[a] - x[b]
            sums[MEMBERS + e] = sums[MEMBERS + e] + lw * d * d
        return tuple(sums)

    sums = (jnp.zeros((8, LANES), F32),) * ENTRIES
    for c, (lo, hi) in enumerate(CHUNKS):
        wait_for(xs.at[:, rows_of(c)], part_recv.at[c])
        sums = lax.fori_loop(lo, hi, add, sums)

    message = jnp.zeros((8, LANES), F32)
    for e in range(0, ENTRIES, 8):
        column = [jnp.sum(s, axis=0, keepdims=True) for s in sums[e : e + 8]]
        column += [jnp.zeros((1, LANES), F32)] * (8 - len(column))
        total = jnp.sum(jnp.concatenate(column, axis=0), axis=1, keepdims=True)
        message = jnp.where(lane == e // 8, total, message)

    def add_over(axes, message, buffer, send, recv):
        place = functools.reduce(lambda at, a: at * AXES[a] + here[a], axes, 0)
        buffer[place] = message
        count = buffer.shape[0]
        for way in steps(axes):
            pltpu.make_async_remote_copy(
                src_ref=buffer.at[place],
                dst_ref=buffer.at[place],
                send_sem=send,
                recv_sem=recv,
                device_id=moved(**way),
                device_id_type=MESH,
            ).start()
        wait_for(buffer.at[pl.ds(0, count - 1)], recv)
        total = buffer[0]
        for i in range(1, count):
            total = total + buffer[i]
        return total

    message = add_over(STAGES[0], message, first, first_send, first_recv)
    message = add_over(STAGES[1], message, second, second_send, second_recv)

    scale = 1.0 / (rows * half * GRID)
    distance = jnp.sqrt(message * scale + 1e-06)
    entry = lane * 8 + sub
    is_truth = entry < MEMBERS
    share_of = jnp.where(is_truth, 1.0 / MEMBERS, -1.0 / (MEMBERS * (MEMBERS - 1)))
    loss[...] = jnp.sum(jnp.where(entry < ENTRIES, distance * share_of, 0.0), keepdims=True)
    loss_copy = pltpu.make_async_copy(loss, loss_out, loss_sem)
    loss_copy.start()
    factor = jnp.where(is_truth, 1.0, 1.0 / (MEMBERS - 1)) / distance
    for e in range(ENTRIES):
        coef[e] = jnp.broadcast_to(factor[e % 8 : e % 8 + 1, e // 8 : e // 8 + 1], (8, LANES))

    back = share // RETURNS

    def back_rows(c):
        return pl.ds(c * back, back)

    def place_of(c):
        return out.at[pl.ds(row0 + c * back, back), pl.ds(pl.multiple_of(side * 8, 8), 8)]

    def res_copy(c, i):
        peer = member_peer(i)
        return pltpu.make_async_remote_copy(
            src_ref=result.at[peer["member"], back_rows(c)],
            dst_ref=place_of(c),
            send_sem=res_send,
            recv_sem=res_recv,
            device_id=peer,
            device_id_type=MESH,
        )

    def keep_copy(c):
        return pltpu.make_async_copy(result.at[m, back_rows(c)], place_of(c), res_recv)

    def derive(n):
        x, y, lw = load_row(n)
        o = [(x[k] - y) * coef[k] for k in range(MEMBERS)]
        for e, (a, b) in enumerate(PAIRS):
            d = (x[a] - x[b]) * coef[MEMBERS + e]
            o[a] = o[a] - d
            o[b] = o[b] + d
        for k in range(MEMBERS):
            result[k, n] = lw * o[k]

    def send_back(c):
        repeat(c * back, c * back + back, derive)
        for i in range(MEMBERS - 1):
            res_copy(c, i).start()
        keep_copy(c).start()

    repeat(0, RETURNS, send_back)

    wait_for(edge_out, edge_send)
    wait_for(parts.at[pl.ds(0, MEMBERS - 1)], part_send)
    y_copy.wait_send()
    wait_for(first.at[pl.ds(0, first.shape[0] - 1)], first_send)
    wait_for(second.at[pl.ds(0, second.shape[0] - 1)], second_send)
    loss_copy.wait()
    wait_for(result.at[pl.ds(0, MEMBERS - 1)], res_send)
    wait_for(out, res_recv)


def local(prediction, reference_state, penalty, area, starts):
    rows, slots = prediction.shape[1:]
    tiles = slots // LANES
    share = rows // GROUPS
    spread = -(-(share + GROUPS - 1) // 8) * 8
    vmem = functools.partial(pltpu.VMEM, dtype=F32)
    array = functools.partial(jax.ShapeDtypeStruct, dtype=F32)
    dma = pltpu.SemaphoreType.DMA
    anywhere = pl.BlockSpec(memory_space=pl.ANY)
    fields = (MEMBERS, share, 8, LANES)
    edges = (SIDES, GROUPS, share, 8, LANES)
    runs = len(CHUNKS)
    y_share = (share + 1, 8, LANES)
    result, loss = pl.pallas_call(
        kernel,
        name="energy_score",
        out_shape=(pltpu.VMEM((rows, tiles // 2, LANES), F32), array((1, 1))),
        in_specs=[anywhere] * 5,
        out_specs=(anywhere, anywhere),
        scratch_shapes=[
            pltpu.SMEM(starts.shape, jnp.int32),
            pltpu.SMEM(penalty.shape, F32),
            vmem((1, 1)),
            vmem((GROUPS, share, tiles, LANES)),
            vmem((rows, slots)),
            vmem((tiles, LANES)),
            vmem((spread * tiles, LANES)),
            vmem(edges),
            vmem(edges),
            vmem(fields),
            vmem(fields),
            vmem(y_share),
            vmem(y_share),
            vmem(y_share),
            vmem(fields),
            vmem((math.prod(AXES[a] for a in STAGES[0]), 8, LANES)),
            vmem((math.prod(AXES[a] for a in STAGES[1]), 8, LANES)),
            vmem((ENTRIES, 8, LANES)),
            dma((runs + 4,)),
            dma,
            dma((runs,)),
            dma,
            dma,
            dma,
            dma((runs,)),
            dma,
            dma,
            dma,
            dma,
            dma,
            dma,
            dma,
        ],
        compiler_params=pltpu.CompilerParams(
            collective_id=0, has_side_effects=True, vmem_limit_bytes=VMEM_BYTES
        ),
    )(
        starts,
        penalty,
        prediction.reshape(GROUPS, share, tiles, LANES),
        reference_state,
        area.reshape(tiles, LANES),
    )
    return (result.reshape(1, rows, slots // 2), loss.reshape(()))


def solution(mesh):
    placed = (P("member", None, "grid"), P(None, "grid"), P(), P("grid"), P())
    return jax.shard_map(
        local,
        mesh=mesh,
        in_specs=placed,
        out_specs=(P("member", None, "grid"), P()),
        check_vma=False,
    )
```

```python
import functools
import itertools
import math

import jax
import jax.numpy as jnp
from jax import lax
from jax.experimental import pallas as pl
from jax.experimental.pallas import tpu as pltpu
from jax.sharding import PartitionSpec as P

MESH = pl.DeviceIdType.MESH
F32 = jnp.float32
LANES = 128
VMEM_BYTES = 56 * 2**20
CHUNKS = ((0, 3), (3, 7), (7, 11), (11, 15), (15, 19), (19, 22), (22, 25))
RETURNS = 5
NX, NZ = 4, 8
NY, NC = 4, 2
MEMBERS = 8
GRID = 32
SIDES = 2
GROUPS = MEMBERS // SIDES
PAIRS = [(a, b) for a in range(MEMBERS) for b in range(a + 1, MEMBERS)]
ENTRIES = MEMBERS + len(PAIRS)


AXES = {"z": NZ, "y": NY, "x": NX, "core": NC}
STAGES = (("z", "core"), ("y", "x"))


def hops(step):
    return sum(min(step[a], AXES[a] - step[a]) for a in step)


def steps(axes):
    ways = itertools.product(*(range(AXES[a]) for a in axes))
    ways = [dict(zip(axes, way)) for way in ways if any(way)]
    return sorted(ways, key=lambda way: -hops(way))


MEMBER_STEPS = ((0, 1), (2, 0), (1, 0), (3, 0), (2, 1), (1, 1), (3, 1))
MEET = [dict(y=y, core=core) for y, core in MEMBER_STEPS]
for axes in STAGES:
    MEET += [way for way in steps(axes) if set(k for k in way if way[k]) - {"y", "core"}]


def repeat(first, end, body):
    def step(i, carry):
        body(i)
        return carry

    lax.fori_loop(first, end, step, 0)


def wait_for(ref, sem):
    pltpu.make_async_copy(ref, ref, sem).wait()


def kernel(
    starts_in,
    penalty_in,
    pred,
    truth,
    area,
    out,
    loss_out,
    starts,
    penalty,
    loss,
    xin,
    yin,
    win,
    y_rows,
    edge_out,
    edge_in,
    parts,
    xs,
    y_out,
    y_in,
    y_own,
    result,
    first,
    second,
    coef,
    load_sem,
    edge_send,
    edge_recv,
    y_send,
    y_recv,
    part_send,
    part_recv,
    first_send,
    first_recv,
    second_send,
    second_recv,
    res_send,
    res_recv,
    loss_sem,
):
    share, tiles = pred.shape[1], pred.shape[2]
    rows = share * GROUPS
    edge = tiles // 4 * LANES
    half = 2 * edge
    m = lax.axis_index("member")
    g = lax.axis_index("grid")
    my, mc = m // NC, m % NC
    gx, gz = g // NZ, g % NZ
    side, group = m % SIDES, m // SIDES
    row0 = group * share

    def moved(z=0, y=0, x=0, core=0):
        member = ((my + y) % NY) * NC + (mc + core) % NC
        return {"member": member, "grid": ((gx + x) % NX) * NZ + (gz + z) % NZ}

    def member_peer(i):
        y, core = MEMBER_STEPS[i]
        y = (y + mc * (NY - 2 * y)) % NY
        return moved(y=y, core=core)

    def grid_peer(step):
        return {"member": m, "grid": (g + step + GRID) % GRID}

    here = {"z": gz, "y": my, "x": gx, "core": mc}
    meet = [(hops(way), moved(**way)) for way in MEET]
    meet += [(2, grid_peer(1)), (2, grid_peer(-1))]
    barrier = pltpu.get_barrier_semaphore()
    for _, peer in sorted(meet, key=lambda entry: -entry[0]):
        pl.semaphore_signal(barrier, inc=1, device_id=peer, device_id_type=MESH)

    def rows_of(c):
        lo, hi = CHUNKS[c]
        return pl.ds(lo, hi - lo)

    def x_load(c):
        return pltpu.make_async_copy(
            pred.at[:, rows_of(c)], xin.at[:, rows_of(c)], load_sem.at[c]
        )

    y_load = pltpu.make_async_copy(truth, yin, load_sem.at[len(CHUNKS)])
    w_load = pltpu.make_async_copy(area, win, load_sem.at[len(CHUNKS) + 1])
    starts_load = pltpu.make_async_copy(starts_in, starts, load_sem.at[len(CHUNKS) + 2])
    penalty_load = pltpu.make_async_copy(penalty_in, penalty, load_sem.at[len(CHUNKS) + 3])
    starts_load.start()
    for c in range(len(CHUNKS)):
        x_load(c).start()
    for copy in (y_load, w_load, penalty_load):
        copy.start()

    starts_load.wait()
    lo_cell = starts[g] - g * half
    hi_cell = starts[g + 1] - g * half
    shift = lo_cell + edge
    whole = lax.div(shift, LANES)
    part = lax.rem(shift, LANES)
    lane = lax.broadcasted_iota(jnp.int32, (8, LANES), 1)
    wrapped = lax.broadcasted_iota(jnp.int32, (tiles, LANES), 1) >= LANES - part

    def aligned(row):
        now = pltpu.roll(row, whole, 0)
        row = pltpu.roll(jnp.where(wrapped, pltpu.roll(now, 1, 0), now), part, 1)
        return [row[i : i + 8] for i in range(0, tiles, 8)]

    sub = lax.broadcasted_iota(jnp.int32, (8, LANES), 0)

    def edge_copy(c, s):
        where = (s, slice(None), rows_of(c))
        return pltpu.make_async_remote_copy(
            src_ref=edge_out.at[where],
            dst_ref=edge_in.at[where],
            send_sem=edge_send,
            recv_sem=edge_recv.at[c],
            device_id=grid_peer(1 if s == 0 else -1),
            device_id_type=MESH,
        )

    y_copy = pltpu.make_async_remote_copy(
        src_ref=y_out,
        dst_ref=y_in,
        send_sem=y_send,
        recv_sem=y_recv,
        device_id={"member": m, "grid": (g + 1 + side * (GRID - 2)) % GRID},
        device_id_type=MESH,
    )

    def part_copy(c, i):
        peer = member_peer(i)
        return pltpu.make_async_remote_copy(
            src_ref=parts.at[peer["member"], rows_of(c)],
            dst_ref=xs.at[m, rows_of(c)],
            send_sem=part_send,
            recv_sem=part_recv.at[c],
            device_id=peer,
            device_id_type=MESH,
        )

    def own_copy(c):
        return pltpu.make_async_copy(
            parts.at[m, rows_of(c)], xs.at[m, rows_of(c)], part_recv.at[c]
        )

    def send_parts(c):
        for i in range(MEMBERS - 1):
            part_copy(c, i).start()
        own_copy(c).start()

    def align(n):
        for k in range(GROUPS):
            before, left, right, after = aligned(xin[k, n])
            edge_out[0, k, n] = after
            edge_out[1, k, n] = before
            parts[SIDES * k, n] = left
            parts[SIDES * k + 1, n] = right

    for c, (lo, hi) in enumerate(CHUNKS):
        x_load(c).wait()
        repeat(lo, hi, align)
        if c == 0:
            pl.semaphore_wait(barrier, len(meet))
        for s in range(SIDES):
            edge_copy(c, s).start()

    y_load.wait()
    w_load.wait()
    full = rows // 8 * 8
    spread = y_rows.shape[0] // tiles - 1

    def turn(t):
        cols = pl.ds(pl.multiple_of(t * LANES, LANES), LANES)
        for n in range(0, spread, 8):
            r = pl.multiple_of(jnp.minimum(row0 - group + n, full - 8), 8)
            value = yin[pl.ds(r, 8), cols]
            if n + 8 == spread:
                rest = jnp.zeros((8 + full - rows, LANES), F32)
                tail = jnp.concatenate([yin[pl.ds(full, rows - full), cols], rest], axis=0)
                value = jnp.where(group == GROUPS - 1, tail, value)
            y_rows[pl.ds(n * tiles + t, 8, stride=tiles), :] = value

    repeat(0, tiles, turn)

    def put_truth(n, row):
        before, left, right, after = aligned(row)
        y_out[n] = jnp.where(side == 0, after, before)
        y_own[n] = jnp.where(side == 0, left, right)

    def align_truth(n):
        put_truth(n, y_rows[pl.ds(pl.multiple_of((group + n) * tiles, tiles), tiles), :])

    repeat(0, share, align_truth)
    put_truth(share, win[...])
    y_copy.start()

    def owned(s):
        cell = s * edge + sub * LANES + lane
        return (cell >= lo_cell) & (cell < hi_cell)

    in_half = [owned(0), owned(1)]

    def merge(n):
        for k in range(MEMBERS):
            s = k % SIDES
            parts[k, n] = jnp.where(in_half[s], parts[k, n], edge_in[s, k // SIDES, n])

    for c, (lo, hi) in enumerate(CHUNKS):
        wait_for(edge_in.at[:, :, rows_of(c)], edge_recv.at[c])
        repeat(lo, hi, merge)
        send_parts(c)

    y_copy.wait_recv()
    in_own = owned(side)

    def merge_truth(n):
        y_own[n] = jnp.where(in_own, y_own[n], y_in[n])

    repeat(0, share + 1, merge_truth)
    own_area = y_own[share]

    def load_row(n):
        x = [xs[k, n] for k in range(MEMBERS)]
        y = y_own[n]
        return x, y, penalty[row0 + n] * own_area

    penalty_load.wait()

    def add(n, sums):
        sums = list(sums)
        x, y, lw = load_row(n)
        for k in range(MEMBERS):
            d = x[k] - y
            sums[k] = sums[k] + lw * d * d
        for e, (a, b) in enumerate(PAIRS):
            d = x[a] - x[b]
            sums[MEMBERS + e] = sums[MEMBERS + e] + lw * d * d
        return tuple(sums)

    sums = (jnp.zeros((8, LANES), F32),) * ENTRIES
    for c, (lo, hi) in enumerate(CHUNKS):
        wait_for(xs.at[:, rows_of(c)], part_recv.at[c])
        sums = lax.fori_loop(lo, hi, add, sums)

    message = jnp.zeros((8, LANES), F32)
    for e in range(0, ENTRIES, 8):
        column = [jnp.sum(s, axis=0, keepdims=True) for s in sums[e : e + 8]]
        column += [jnp.zeros((1, LANES), F32)] * (8 - len(column))
        total = jnp.sum(jnp.concatenate(column, axis=0), axis=1, keepdims=True)
        message = jnp.where(lane == e // 8, total, message)

    def add_over(axes, message, buffer, send, recv):
        place = functools.reduce(lambda at, a: at * AXES[a] + here[a], axes, 0)
        buffer[place] = message
        count = buffer.shape[0]
        for way in steps(axes):
            pltpu.make_async_remote_copy(
                src_ref=buffer.at[place],
                dst_ref=buffer.at[place],
                send_sem=send,
                recv_sem=recv,
                device_id=moved(**way),
                device_id_type=MESH,
            ).start()
        wait_for(buffer.at[pl.ds(0, count - 1)], recv)
        total = buffer[0]
        for i in range(1, count):
            total = total + buffer[i]
        return total

    message = add_over(STAGES[0], message, first, first_send, first_recv)
    message = add_over(STAGES[1], message, second, second_send, second_recv)

    scale = 1.0 / (rows * half * GRID)
    distance = jnp.sqrt(message * scale + 1e-06)
    entry = lane * 8 + sub
    is_truth = entry < MEMBERS
    share_of = jnp.where(is_truth, 1.0 / MEMBERS, -1.0 / (MEMBERS * (MEMBERS - 1)))
    loss[...] = jnp.sum(jnp.where(entry < ENTRIES, distance * share_of, 0.0), keepdims=True)
    loss_copy = pltpu.make_async_copy(loss, loss_out, loss_sem)
    loss_copy.start()
    factor = jnp.where(is_truth, 1.0, 1.0 / (MEMBERS - 1)) / distance
    for e in range(ENTRIES):
        coef[e] = jnp.broadcast_to(factor[e % 8 : e % 8 + 1, e // 8 : e // 8 + 1], (8, LANES))

    back = share // RETURNS

    def back_rows(c):
        return pl.ds(c * back, back)

    def place_of(c):
        return out.at[pl.ds(row0 + c * back, back), pl.ds(pl.multiple_of(side * 8, 8), 8)]

    def res_copy(c, i):
        peer = member_peer(i)
        return pltpu.make_async_remote_copy(
            src_ref=result.at[peer["member"], back_rows(c)],
            dst_ref=place_of(c),
            send_sem=res_send,
            recv_sem=res_recv,
            device_id=peer,
            device_id_type=MESH,
        )

    def keep_copy(c):
        return pltpu.make_async_copy(result.at[m, back_rows(c)], place_of(c), res_recv)

    def derive(n):
        x, y, lw = load_row(n)
        o = [(x[k] - y) * coef[k] for k in range(MEMBERS)]
        for e, (a, b) in enumerate(PAIRS):
            d = (x[a] - x[b]) * coef[MEMBERS + e]
            o[a] = o[a] - d
            o[b] = o[b] + d
        for k in range(MEMBERS):
            result[k, n] = lw * o[k]

    def send_back(c):
        repeat(c * back, c * back + back, derive)
        for i in range(MEMBERS - 1):
            res_copy(c, i).start()
        keep_copy(c).start()

    repeat(0, RETURNS, send_back)

    wait_for(edge_out, edge_send)
    wait_for(parts.at[pl.ds(0, MEMBERS - 1)], part_send)
    y_copy.wait_send()
    wait_for(first.at[pl.ds(0, first.shape[0] - 1)], first_send)
    wait_for(second.at[pl.ds(0, second.shape[0] - 1)], second_send)
    loss_copy.wait()
    wait_for(result.at[pl.ds(0, MEMBERS - 1)], res_send)
    wait_for(out, res_recv)


def local(prediction, reference_state, penalty, area, starts):
    rows, slots = prediction.shape[1:]
    tiles = slots // LANES
    share = rows // GROUPS
    spread = -(-(share + GROUPS - 1) // 8) * 8
    vmem = functools.partial(pltpu.VMEM, dtype=F32)
    array = functools.partial(jax.ShapeDtypeStruct, dtype=F32)
    dma = pltpu.SemaphoreType.DMA
    anywhere = pl.BlockSpec(memory_space=pl.ANY)
    fields = (MEMBERS, share, 8, LANES)
    edges = (SIDES, GROUPS, share, 8, LANES)
    runs = len(CHUNKS)
    y_share = (share + 1, 8, LANES)
    result, loss = pl.pallas_call(
        kernel,
        name="energy_score",
        out_shape=(pltpu.VMEM((rows, tiles // 2, LANES), F32), array((1, 1))),
        in_specs=[anywhere] * 5,
        out_specs=(anywhere, anywhere),
        scratch_shapes=[
            pltpu.SMEM(starts.shape, jnp.int32),
            pltpu.SMEM(penalty.shape, F32),
            vmem((1, 1)),
            vmem((GROUPS, share, tiles, LANES)),
            vmem((rows, slots)),
            vmem((tiles, LANES)),
            vmem(((spread + 1) * tiles, LANES)),
            vmem(edges),
            vmem(edges),
            vmem(fields),
            vmem(fields),
            vmem(y_share),
            vmem(y_share),
            vmem(y_share),
            vmem(fields),
            vmem((math.prod(AXES[a] for a in STAGES[0]), 8, LANES)),
            vmem((math.prod(AXES[a] for a in STAGES[1]), 8, LANES)),
            vmem((ENTRIES, 8, LANES)),
            dma((runs + 4,)),
            dma,
            dma((runs,)),
            dma,
            dma,
            dma,
            dma((runs,)),
            dma,
            dma,
            dma,
            dma,
            dma,
            dma,
            dma,
        ],
        compiler_params=pltpu.CompilerParams(
            collective_id=0, has_side_effects=True, vmem_limit_bytes=VMEM_BYTES
        ),
    )(
        starts,
        penalty,
        prediction.reshape(GROUPS, share, tiles, LANES),
        reference_state,
        area.reshape(tiles, LANES),
    )
    return (result.reshape(1, rows, slots // 2), loss.reshape(()))


def solution(mesh):
    placed = (P("member", None, "grid"), P(None, "grid"), P(), P("grid"), P())
    return jax.shard_map(
        local,
        mesh=mesh,
        in_specs=placed,
        out_specs=(P("member", None, "grid"), P()),
        check_vma=False,
    )
```

```python
import functools
import itertools
import math

import jax
import jax.numpy as jnp
from jax import lax
from jax.experimental import pallas as pl
from jax.experimental.pallas import tpu as pltpu
from jax.sharding import PartitionSpec as P

MESH = pl.DeviceIdType.MESH
F32 = jnp.float32
LANES = 128
VMEM_BYTES = 56 * 2**20
CHUNKS = ((0, 3), (3, 7), (7, 11), (11, 15), (15, 19), (19, 22), (22, 25))
RETURNS = 5
NX, NZ = 4, 8
NY, NC = 4, 2
MEMBERS = 8
GRID = 32
SIDES = 2
GROUPS = MEMBERS // SIDES
PAIRS = [(a, b) for a in range(MEMBERS) for b in range(a + 1, MEMBERS)]
ENTRIES = MEMBERS + len(PAIRS)


AXES = {"z": NZ, "y": NY, "x": NX, "core": NC}
STAGES = (("z", "core"), ("y", "x"))


def hops(step):
    return sum(min(step[a], AXES[a] - step[a]) for a in step)


def steps(axes):
    ways = itertools.product(*(range(AXES[a]) for a in axes))
    ways = [dict(zip(axes, way)) for way in ways if any(way)]
    return sorted(ways, key=lambda way: -hops(way))


MEMBER_STEPS = ((0, 1), (2, 0), (1, 0), (3, 0), (2, 1), (1, 1), (3, 1))
MEET = [dict(y=y, core=core) for y, core in MEMBER_STEPS]
MEET += [dict(x=x) for x in range(1, NX)] + [dict(z=1), dict(z=NZ - 1)]
RELAY_AFTER = (1, 3, 6)
RELAYS = NZ // 2 - 1


def repeat(first, end, body):
    def step(i, carry):
        body(i)
        return carry

    lax.fori_loop(first, end, step, 0)


def wait_for(ref, sem):
    pltpu.make_async_copy(ref, ref, sem).wait()


def kernel(
    starts_in,
    penalty_in,
    pred,
    truth,
    area,
    out,
    loss_out,
    starts,
    penalty,
    loss,
    xin,
    yin,
    win,
    y_rows,
    edge_out,
    edge_in,
    parts,
    xs,
    y_out,
    y_in,
    y_own,
    result,
    first,
    second,
    coef,
    load_sem,
    edge_send,
    edge_recv,
    y_send,
    y_recv,
    part_send,
    part_recv,
    first_send,
    first_recv,
    second_send,
    second_recv,
    res_send,
    res_recv,
    loss_sem,
    relay,
):
    share, tiles = pred.shape[1], pred.shape[2]
    rows = share * GROUPS
    edge = tiles // 4 * LANES
    half = 2 * edge
    m = lax.axis_index("member")
    g = lax.axis_index("grid")
    my, mc = m // NC, m % NC
    gx, gz = g // NZ, g % NZ
    side, group = m % SIDES, m // SIDES
    row0 = group * share

    def moved(z=0, y=0, x=0, core=0):
        member = ((my + y) % NY) * NC + (mc + core) % NC
        return {"member": member, "grid": ((gx + x) % NX) * NZ + (gz + z) % NZ}

    def member_peer(i):
        y, core = MEMBER_STEPS[i]
        y = (y + mc * (NY - 2 * y)) % NY
        return moved(y=y, core=core)

    def grid_peer(step):
        return {"member": m, "grid": (g + step + GRID) % GRID}

    here = {"z": gz, "y": my, "x": gx, "core": mc}
    meet = [(hops(way), moved(**way)) for way in MEET]
    meet += [(2, grid_peer(1)), (2, grid_peer(-1))]
    barrier = pltpu.get_barrier_semaphore()
    for _, peer in sorted(meet, key=lambda entry: -entry[0]):
        pl.semaphore_signal(barrier, inc=1, device_id=peer, device_id_type=MESH)

    def pass_on(i):
        for z in (1, NZ - 1):
            pl.semaphore_signal(relay.at[i], inc=1, device_id=moved(z=z), device_id_type=MESH)

    def rows_of(c):
        lo, hi = CHUNKS[c]
        return pl.ds(lo, hi - lo)

    def x_load(c):
        return pltpu.make_async_copy(
            pred.at[:, rows_of(c)], xin.at[:, rows_of(c)], load_sem.at[c]
        )

    y_load = pltpu.make_async_copy(truth, yin, load_sem.at[len(CHUNKS)])
    w_load = pltpu.make_async_copy(area, win, load_sem.at[len(CHUNKS) + 1])
    starts_load = pltpu.make_async_copy(starts_in, starts, load_sem.at[len(CHUNKS) + 2])
    penalty_load = pltpu.make_async_copy(penalty_in, penalty, load_sem.at[len(CHUNKS) + 3])
    starts_load.start()
    for c in range(len(CHUNKS)):
        x_load(c).start()
    for copy in (y_load, w_load, penalty_load):
        copy.start()

    starts_load.wait()
    lo_cell = starts[g] - g * half
    hi_cell = starts[g + 1] - g * half
    shift = lo_cell + edge
    whole = lax.div(shift, LANES)
    part = lax.rem(shift, LANES)
    lane = lax.broadcasted_iota(jnp.int32, (8, LANES), 1)
    wrapped = lax.broadcasted_iota(jnp.int32, (tiles, LANES), 1) >= LANES - part

    def aligned(row):
        now = pltpu.roll(row, whole, 0)
        row = pltpu.roll(jnp.where(wrapped, pltpu.roll(now, 1, 0), now), part, 1)
        return [row[i : i + 8] for i in range(0, tiles, 8)]

    sub = lax.broadcasted_iota(jnp.int32, (8, LANES), 0)

    def edge_copy(c, s):
        where = (s, slice(None), rows_of(c))
        return pltpu.make_async_remote_copy(
            src_ref=edge_out.at[where],
            dst_ref=edge_in.at[where],
            send_sem=edge_send,
            recv_sem=edge_recv.at[c],
            device_id=grid_peer(1 if s == 0 else -1),
            device_id_type=MESH,
        )

    y_copy = pltpu.make_async_remote_copy(
        src_ref=y_out,
        dst_ref=y_in,
        send_sem=y_send,
        recv_sem=y_recv,
        device_id={"member": m, "grid": (g + 1 + side * (GRID - 2)) % GRID},
        device_id_type=MESH,
    )

    def part_copy(c, i):
        peer = member_peer(i)
        return pltpu.make_async_remote_copy(
            src_ref=parts.at[peer["member"], rows_of(c)],
            dst_ref=xs.at[m, rows_of(c)],
            send_sem=part_send,
            recv_sem=part_recv.at[c],
            device_id=peer,
            device_id_type=MESH,
        )

    def own_copy(c):
        return pltpu.make_async_copy(
            parts.at[m, rows_of(c)], xs.at[m, rows_of(c)], part_recv.at[c]
        )

    def send_parts(c):
        for i in range(MEMBERS - 1):
            part_copy(c, i).start()
        own_copy(c).start()

    def align(n):
        for k in range(GROUPS):
            before, left, right, after = aligned(xin[k, n])
            edge_out[0, k, n] = after
            edge_out[1, k, n] = before
            parts[SIDES * k, n] = left
            parts[SIDES * k + 1, n] = right

    for c, (lo, hi) in enumerate(CHUNKS):
        x_load(c).wait()
        repeat(lo, hi, align)
        if c == 0:
            pl.semaphore_wait(barrier, len(meet))
            pass_on(0)
        for s in range(SIDES):
            edge_copy(c, s).start()

    y_load.wait()
    w_load.wait()
    full = rows // 8 * 8
    spread = y_rows.shape[0] // tiles - 1

    def turn(t):
        cols = pl.ds(pl.multiple_of(t * LANES, LANES), LANES)
        for n in range(0, spread, 8):
            r = pl.multiple_of(jnp.minimum(row0 - group + n, full - 8), 8)
            value = yin[pl.ds(r, 8), cols]
            if n + 8 == spread:
                rest = jnp.zeros((8 + full - rows, LANES), F32)
                tail = jnp.concatenate([yin[pl.ds(full, rows - full), cols], rest], axis=0)
                value = jnp.where(group == GROUPS - 1, tail, value)
            y_rows[pl.ds(n * tiles + t, 8, stride=tiles), :] = value

    repeat(0, tiles, turn)

    def put_truth(n, row):
        before, left, right, after = aligned(row)
        y_out[n] = jnp.where(side == 0, after, before)
        y_own[n] = jnp.where(side == 0, left, right)

    def align_truth(n):
        put_truth(n, y_rows[pl.ds(pl.multiple_of((group + n) * tiles, tiles), tiles), :])

    repeat(0, share, align_truth)
    put_truth(share, win[...])
    y_copy.start()

    def owned(s):
        cell = s * edge + sub * LANES + lane
        return (cell >= lo_cell) & (cell < hi_cell)

    in_half = [owned(0), owned(1)]

    def merge(n):
        for k in range(MEMBERS):
            s = k % SIDES
            parts[k, n] = jnp.where(in_half[s], parts[k, n], edge_in[s, k // SIDES, n])

    for c, (lo, hi) in enumerate(CHUNKS):
        wait_for(edge_in.at[:, :, rows_of(c)], edge_recv.at[c])
        repeat(lo, hi, merge)
        if c in RELAY_AFTER:
            i = RELAY_AFTER.index(c)
            pl.semaphore_wait(relay.at[i], 2)
            if i + 1 < RELAYS:
                pass_on(i + 1)
        send_parts(c)

    y_copy.wait_recv()
    in_own = owned(side)

    def merge_truth(n):
        y_own[n] = jnp.where(in_own, y_own[n], y_in[n])

    repeat(0, share + 1, merge_truth)
    own_area = y_own[share]

    def load_row(n):
        x = [xs[k, n] for k in range(MEMBERS)]
        y = y_own[n]
        return x, y, penalty[row0 + n] * own_area

    penalty_load.wait()

    def add(n, sums):
        sums = list(sums)
        x, y, lw = load_row(n)
        for k in range(MEMBERS):
            d = x[k] - y
            sums[k] = sums[k] + lw * d * d
        for e, (a, b) in enumerate(PAIRS):
            d = x[a] - x[b]
            sums[MEMBERS + e] = sums[MEMBERS + e] + lw * d * d
        return tuple(sums)

    sums = (jnp.zeros((8, LANES), F32),) * ENTRIES
    for c, (lo, hi) in enumerate(CHUNKS):
        wait_for(xs.at[:, rows_of(c)], part_recv.at[c])
        sums = lax.fori_loop(lo, hi, add, sums)

    message = jnp.zeros((8, LANES), F32)
    for e in range(0, ENTRIES, 8):
        column = [jnp.sum(s, axis=0, keepdims=True) for s in sums[e : e + 8]]
        column += [jnp.zeros((1, LANES), F32)] * (8 - len(column))
        total = jnp.sum(jnp.concatenate(column, axis=0), axis=1, keepdims=True)
        message = jnp.where(lane == e // 8, total, message)

    def add_over(axes, message, buffer, send, recv):
        place = functools.reduce(lambda at, a: at * AXES[a] + here[a], axes, 0)
        buffer[place] = message
        count = buffer.shape[0]
        for way in steps(axes):
            pltpu.make_async_remote_copy(
                src_ref=buffer.at[place],
                dst_ref=buffer.at[place],
                send_sem=send,
                recv_sem=recv,
                device_id=moved(**way),
                device_id_type=MESH,
            ).start()
        wait_for(buffer.at[pl.ds(0, count - 1)], recv)
        total = buffer[0]
        for i in range(1, count):
            total = total + buffer[i]
        return total

    message = add_over(STAGES[0], message, first, first_send, first_recv)
    message = add_over(STAGES[1], message, second, second_send, second_recv)

    scale = 1.0 / (rows * half * GRID)
    distance = jnp.sqrt(message * scale + 1e-06)
    entry = lane * 8 + sub
    is_truth = entry < MEMBERS
    share_of = jnp.where(is_truth, 1.0 / MEMBERS, -1.0 / (MEMBERS * (MEMBERS - 1)))
    loss[...] = jnp.sum(jnp.where(entry < ENTRIES, distance * share_of, 0.0), keepdims=True)
    loss_copy = pltpu.make_async_copy(loss, loss_out, loss_sem)
    loss_copy.start()
    factor = jnp.where(is_truth, 1.0, 1.0 / (MEMBERS - 1)) / distance
    for e in range(ENTRIES):
        coef[e] = jnp.broadcast_to(factor[e % 8 : e % 8 + 1, e // 8 : e // 8 + 1], (8, LANES))

    back = share // RETURNS

    def back_rows(c):
        return pl.ds(c * back, back)

    def place_of(c):
        return out.at[pl.ds(row0 + c * back, back), pl.ds(pl.multiple_of(side * 8, 8), 8)]

    def res_copy(c, i):
        peer = member_peer(i)
        return pltpu.make_async_remote_copy(
            src_ref=result.at[peer["member"], back_rows(c)],
            dst_ref=place_of(c),
            send_sem=res_send,
            recv_sem=res_recv,
            device_id=peer,
            device_id_type=MESH,
        )

    def keep_copy(c):
        return pltpu.make_async_copy(result.at[m, back_rows(c)], place_of(c), res_recv)

    def derive(n):
        x, y, lw = load_row(n)
        o = [(x[k] - y) * coef[k] for k in range(MEMBERS)]
        for e, (a, b) in enumerate(PAIRS):
            d = (x[a] - x[b]) * coef[MEMBERS + e]
            o[a] = o[a] - d
            o[b] = o[b] + d
        for k in range(MEMBERS):
            result[k, n] = lw * o[k]

    def send_back(c):
        repeat(c * back, c * back + back, derive)
        for i in range(MEMBERS - 1):
            res_copy(c, i).start()
        keep_copy(c).start()

    repeat(0, RETURNS, send_back)

    wait_for(edge_out, edge_send)
    wait_for(parts.at[pl.ds(0, MEMBERS - 1)], part_send)
    y_copy.wait_send()
    wait_for(first.at[pl.ds(0, first.shape[0] - 1)], first_send)
    wait_for(second.at[pl.ds(0, second.shape[0] - 1)], second_send)
    loss_copy.wait()
    wait_for(result.at[pl.ds(0, MEMBERS - 1)], res_send)
    wait_for(out, res_recv)


def local(prediction, reference_state, penalty, area, starts):
    rows, slots = prediction.shape[1:]
    tiles = slots // LANES
    share = rows // GROUPS
    spread = -(-(share + GROUPS - 1) // 8) * 8
    vmem = functools.partial(pltpu.VMEM, dtype=F32)
    array = functools.partial(jax.ShapeDtypeStruct, dtype=F32)
    dma = pltpu.SemaphoreType.DMA
    anywhere = pl.BlockSpec(memory_space=pl.ANY)
    fields = (MEMBERS, share, 8, LANES)
    edges = (SIDES, GROUPS, share, 8, LANES)
    runs = len(CHUNKS)
    y_share = (share + 1, 8, LANES)
    result, loss = pl.pallas_call(
        kernel,
        name="energy_score",
        out_shape=(pltpu.VMEM((rows, tiles // 2, LANES), F32), array((1, 1))),
        in_specs=[anywhere] * 5,
        out_specs=(anywhere, anywhere),
        scratch_shapes=[
            pltpu.SMEM(starts.shape, jnp.int32),
            pltpu.SMEM(penalty.shape, F32),
            vmem((1, 1)),
            vmem((GROUPS, share, tiles, LANES)),
            vmem((rows, slots)),
            vmem((tiles, LANES)),
            vmem(((spread + 1) * tiles, LANES)),
            vmem(edges),
            vmem(edges),
            vmem(fields),
            vmem(fields),
            vmem(y_share),
            vmem(y_share),
            vmem(y_share),
            vmem(fields),
            vmem((math.prod(AXES[a] for a in STAGES[0]), 8, LANES)),
            vmem((math.prod(AXES[a] for a in STAGES[1]), 8, LANES)),
            vmem((ENTRIES, 8, LANES)),
            dma((runs + 4,)),
            dma,
            dma((runs,)),
            dma,
            dma,
            dma,
            dma((runs,)),
            dma,
            dma,
            dma,
            dma,
            dma,
            dma,
            dma,
            pltpu.SemaphoreType.REGULAR((RELAYS,)),
        ],
        compiler_params=pltpu.CompilerParams(
            collective_id=0, has_side_effects=True, vmem_limit_bytes=VMEM_BYTES
        ),
    )(
        starts,
        penalty,
        prediction.reshape(GROUPS, share, tiles, LANES),
        reference_state,
        area.reshape(tiles, LANES),
    )
    return (result.reshape(1, rows, slots // 2), loss.reshape(()))


def solution(mesh):
    placed = (P("member", None, "grid"), P(None, "grid"), P(), P("grid"), P())
    return jax.shard_map(
        local,
        mesh=mesh,
        in_specs=placed,
        out_specs=(P("member", None, "grid"), P()),
        check_vma=False,
    )
```

```python
import functools
import itertools
import math

import jax
import jax.numpy as jnp
from jax import lax
from jax.experimental import pallas as pl
from jax.experimental.pallas import tpu as pltpu
from jax.sharding import PartitionSpec as P

MESH = pl.DeviceIdType.MESH
F32 = jnp.float32
LANES = 128
VMEM_BYTES = 56 * 2**20
CHUNKS = ((0, 3), (3, 7), (7, 11), (11, 15), (15, 19), (19, 22), (22, 25))
RETURNS = 5
NX, NZ = 4, 8
NY, NC = 4, 2
MEMBERS = 8
GRID = 32
SIDES = 2
GROUPS = MEMBERS // SIDES
PAIRS = [(a, b) for a in range(MEMBERS) for b in range(a + 1, MEMBERS)]
ENTRIES = MEMBERS + len(PAIRS)


AXES = {"z": NZ, "y": NY, "x": NX, "core": NC}
STAGES = (("z", "core"), ("y", "x"))


def hops(step):
    return sum(min(step[a], AXES[a] - step[a]) for a in step)


def steps(axes):
    ways = itertools.product(*(range(AXES[a]) for a in axes))
    ways = [dict(zip(axes, way)) for way in ways if any(way)]
    return sorted(ways, key=lambda way: -hops(way))


MEMBER_STEPS = ((0, 1), (2, 0), (1, 0), (3, 0), (2, 1), (1, 1), (3, 1))
MEET = [dict(y=y, core=core) for y, core in MEMBER_STEPS]
MEET += [dict(x=x) for x in range(1, NX)] + [dict(z=1), dict(z=NZ - 1)]
RELAY_AFTER = (1, 3, 6)
RELAYS = NZ // 2 - 1


def repeat(first, end, body):
    def step(i, carry):
        body(i)
        return carry

    lax.fori_loop(first, end, step, 0)


def wait_for(ref, sem):
    pltpu.make_async_copy(ref, ref, sem).wait()


def kernel(
    starts_in,
    penalty_in,
    pred,
    truth,
    area,
    out,
    loss_out,
    starts,
    penalty,
    loss,
    xin,
    yin,
    win,
    y_rows,
    edge_out,
    edge_in,
    parts,
    xs,
    y_out,
    y_in,
    y_own,
    result,
    first,
    second,
    coef,
    load_sem,
    edge_send,
    edge_recv,
    y_send,
    y_recv,
    part_send,
    part_recv,
    first_send,
    first_recv,
    second_send,
    second_recv,
    res_send,
    res_recv,
    loss_sem,
    relay,
):
    share, tiles = pred.shape[1], pred.shape[2]
    rows = share * GROUPS
    edge = tiles // 4 * LANES
    half = 2 * edge
    m = lax.axis_index("member")
    g = lax.axis_index("grid")
    my, mc = m // NC, m % NC
    gx, gz = g // NZ, g % NZ
    side, group = m % SIDES, m // SIDES
    row0 = group * share

    def moved(z=0, y=0, x=0, core=0):
        member = ((my + y) % NY) * NC + (mc + core) % NC
        return {"member": member, "grid": ((gx + x) % NX) * NZ + (gz + z) % NZ}

    def member_peer(i):
        y, core = MEMBER_STEPS[i]
        y = (y + mc * (NY - 2 * y)) % NY
        return moved(y=y, core=core)

    def grid_peer(step):
        return {"member": m, "grid": (g + step + GRID) % GRID}

    here = {"z": gz, "y": my, "x": gx, "core": mc}
    meet = [(hops(way), moved(**way)) for way in MEET]
    meet += [(2, grid_peer(1)), (2, grid_peer(-1))]
    barrier = pltpu.get_barrier_semaphore()
    for _, peer in sorted(meet, key=lambda entry: -entry[0]):
        pl.semaphore_signal(barrier, inc=1, device_id=peer, device_id_type=MESH)

    def pass_on(i):
        for z in (1, NZ - 1):
            pl.semaphore_signal(relay.at[i], inc=1, device_id=moved(z=z), device_id_type=MESH)

    def rows_of(c):
        lo, hi = CHUNKS[c]
        return pl.ds(lo, hi - lo)

    def x_load(c):
        return pltpu.make_async_copy(
            pred.at[:, rows_of(c)], xin.at[:, rows_of(c)], load_sem.at[c]
        )

    y_load = pltpu.make_async_copy(truth, yin, load_sem.at[len(CHUNKS)])
    w_load = pltpu.make_async_copy(area, win, load_sem.at[len(CHUNKS) + 1])
    starts_load = pltpu.make_async_copy(starts_in, starts, load_sem.at[len(CHUNKS) + 2])
    penalty_load = pltpu.make_async_copy(penalty_in, penalty, load_sem.at[len(CHUNKS) + 3])
    starts_load.start()
    for c in range(len(CHUNKS)):
        x_load(c).start()
    for copy in (y_load, w_load, penalty_load):
        copy.start()

    starts_load.wait()
    lo_cell = starts[g] - g * half
    hi_cell = starts[g + 1] - g * half
    shift = lo_cell + edge
    whole = lax.div(shift, LANES)
    part = lax.rem(shift, LANES)
    lane = lax.broadcasted_iota(jnp.int32, (8, LANES), 1)
    wrapped = lax.broadcasted_iota(jnp.int32, (tiles, LANES), 1) >= LANES - part

    def aligned(row):
        now = pltpu.roll(row, whole, 0)
        row = pltpu.roll(jnp.where(wrapped, pltpu.roll(now, 1, 0), now), part, 1)
        return [row[i : i + 8] for i in range(0, tiles, 8)]

    sub = lax.broadcasted_iota(jnp.int32, (8, LANES), 0)

    def edge_copy(c, s):
        where = (s, slice(None), rows_of(c))
        return pltpu.make_async_remote_copy(
            src_ref=edge_out.at[where],
            dst_ref=edge_in.at[where],
            send_sem=edge_send,
            recv_sem=edge_recv.at[c],
            device_id=grid_peer(1 if s == 0 else -1),
            device_id_type=MESH,
        )

    y_copy = pltpu.make_async_remote_copy(
        src_ref=y_out,
        dst_ref=y_in,
        send_sem=y_send,
        recv_sem=y_recv,
        device_id={"member": m, "grid": (g + 1 + side * (GRID - 2)) % GRID},
        device_id_type=MESH,
    )

    def part_copy(c, i):
        peer = member_peer(i)
        return pltpu.make_async_remote_copy(
            src_ref=parts.at[peer["member"], rows_of(c)],
            dst_ref=xs.at[m, rows_of(c)],
            send_sem=part_send,
            recv_sem=part_recv.at[c],
            device_id=peer,
            device_id_type=MESH,
        )

    def own_copy(c):
        return pltpu.make_async_copy(
            parts.at[m, rows_of(c)], xs.at[m, rows_of(c)], part_recv.at[c]
        )

    def send_parts(c):
        for i in range(MEMBERS - 1):
            part_copy(c, i).start()
        own_copy(c).start()

    def align(n):
        for k in range(GROUPS):
            before, left, right, after = aligned(xin[k, n])
            edge_out[0, k, n] = after
            edge_out[1, k, n] = before
            parts[SIDES * k, n] = left
            parts[SIDES * k + 1, n] = right

    for c, (lo, hi) in enumerate(CHUNKS):
        x_load(c).wait()
        repeat(lo, hi, align)
        if c == 0:
            pl.semaphore_wait(barrier, len(meet))
            pass_on(0)
        for s in range(SIDES):
            edge_copy(c, s).start()

    y_load.wait()
    w_load.wait()
    full = rows // 8 * 8
    spread = y_rows.shape[0] // tiles - 1

    def turn(t):
        cols = pl.ds(pl.multiple_of(t * LANES, LANES), LANES)
        for n in range(0, spread, 8):
            r = pl.multiple_of(jnp.minimum(row0 - group + n, full - 8), 8)
            value = yin[pl.ds(r, 8), cols]
            if n + 8 == spread:
                rest = jnp.zeros((8 + full - rows, LANES), F32)
                tail = jnp.concatenate([yin[pl.ds(full, rows - full), cols], rest], axis=0)
                value = jnp.where(group == GROUPS - 1, tail, value)
            y_rows[pl.ds(n * tiles + t, 8, stride=tiles), :] = value

    repeat(0, tiles, turn)

    def put_truth(n, row):
        before, left, right, after = aligned(row)
        y_out[n] = jnp.where(side == 0, after, before)
        y_own[n] = jnp.where(side == 0, left, right)

    def align_truth(n):
        put_truth(n, y_rows[pl.ds(pl.multiple_of((group + n) * tiles, tiles), tiles), :])

    repeat(0, share, align_truth)
    put_truth(share, win[...])
    y_copy.start()

    def owned(s):
        cell = s * edge + sub * LANES + lane
        return (cell >= lo_cell) & (cell < hi_cell)

    in_half = [owned(0), owned(1)]

    def merge(n):
        for k in range(MEMBERS):
            s = k % SIDES
            parts[k, n] = jnp.where(in_half[s], parts[k, n], edge_in[s, k // SIDES, n])

    for c, (lo, hi) in enumerate(CHUNKS):
        wait_for(edge_in.at[:, :, rows_of(c)], edge_recv.at[c])
        repeat(lo, hi, merge)
        if c in RELAY_AFTER:
            i = RELAY_AFTER.index(c)
            pl.semaphore_wait(relay.at[i], 2)
            if i + 1 < RELAYS:
                pass_on(i + 1)
        send_parts(c)

    y_copy.wait_recv()
    in_own = owned(side)

    def merge_truth(n):
        y_own[n] = jnp.where(in_own, y_own[n], y_in[n])

    repeat(0, share + 1, merge_truth)
    own_area = y_own[share]

    def load_row(n):
        x = [xs[k, n] for k in range(MEMBERS)]
        y = y_own[n]
        return x, y, penalty[row0 + n] * own_area

    penalty_load.wait()

    def add(n, sums):
        sums = list(sums)
        x, y, lw = load_row(n)
        for k in range(MEMBERS):
            d = x[k] - y
            sums[k] = sums[k] + lw * d * d
        for e, (a, b) in enumerate(PAIRS):
            d = x[a] - x[b]
            sums[MEMBERS + e] = sums[MEMBERS + e] + lw * d * d
        return tuple(sums)

    sums = (jnp.zeros((8, LANES), F32),) * ENTRIES
    for c, (lo, hi) in enumerate(CHUNKS):
        wait_for(xs.at[:, rows_of(c)], part_recv.at[c])
        sums = lax.fori_loop(lo, hi, add, sums)

    message = jnp.zeros((8, LANES), F32)
    for e in range(0, ENTRIES, 8):
        column = [jnp.sum(s, axis=0, keepdims=True) for s in sums[e : e + 8]]
        column += [jnp.zeros((1, LANES), F32)] * (8 - len(column))
        total = jnp.sum(jnp.concatenate(column, axis=0), axis=1, keepdims=True)
        message = jnp.where(lane == e + sub, total, message)
    message = jnp.sum(message, axis=0, keepdims=True)

    def add_over(axes, message, buffer, send, recv):
        place = functools.reduce(lambda at, a: at * AXES[a] + here[a], axes, 0)
        buffer[place] = message
        count = buffer.shape[0]
        for way in steps(axes):
            pltpu.make_async_remote_copy(
                src_ref=buffer.at[place],
                dst_ref=buffer.at[place],
                send_sem=send,
                recv_sem=recv,
                device_id=moved(**way),
                device_id_type=MESH,
            ).start()
        wait_for(buffer.at[pl.ds(0, count - 1)], recv)
        total = buffer[0]
        for i in range(1, count):
            total = total + buffer[i]
        return total

    message = add_over(STAGES[0], message, first, first_send, first_recv)
    message = add_over(STAGES[1], message, second, second_send, second_recv)

    scale = 1.0 / (rows * half * GRID)
    distance = jnp.sqrt(message * scale + 1e-06)
    entry = lane[:1]
    is_truth = entry < MEMBERS
    share_of = jnp.where(is_truth, 1.0 / MEMBERS, -1.0 / (MEMBERS * (MEMBERS - 1)))
    loss[...] = jnp.sum(jnp.where(entry < ENTRIES, distance * share_of, 0.0), keepdims=True)
    loss_copy = pltpu.make_async_copy(loss, loss_out, loss_sem)
    loss_copy.start()
    factor = jnp.where(is_truth, 1.0, 1.0 / (MEMBERS - 1)) / distance
    for e in range(ENTRIES):
        coef[e] = jnp.broadcast_to(factor[:, e : e + 1], (8, LANES))

    back = share // RETURNS

    def back_rows(c):
        return pl.ds(c * back, back)

    def place_of(c):
        return out.at[pl.ds(row0 + c * back, back), pl.ds(pl.multiple_of(side * 8, 8), 8)]

    def res_copy(c, i):
        peer = member_peer(i)
        return pltpu.make_async_remote_copy(
            src_ref=result.at[peer["member"], back_rows(c)],
            dst_ref=place_of(c),
            send_sem=res_send,
            recv_sem=res_recv,
            device_id=peer,
            device_id_type=MESH,
        )

    def keep_copy(c):
        return pltpu.make_async_copy(result.at[m, back_rows(c)], place_of(c), res_recv)

    def derive(n):
        x, y, lw = load_row(n)
        o = [(x[k] - y) * coef[k] for k in range(MEMBERS)]
        for e, (a, b) in enumerate(PAIRS):
            d = (x[a] - x[b]) * coef[MEMBERS + e]
            o[a] = o[a] - d
            o[b] = o[b] + d
        for k in range(MEMBERS):
            result[k, n] = lw * o[k]

    def send_back(c):
        repeat(c * back, c * back + back, derive)
        for i in range(MEMBERS - 1):
            res_copy(c, i).start()
        keep_copy(c).start()

    repeat(0, RETURNS, send_back)

    wait_for(edge_out, edge_send)
    wait_for(parts.at[pl.ds(0, MEMBERS - 1)], part_send)
    y_copy.wait_send()
    wait_for(first.at[pl.ds(0, first.shape[0] - 1)], first_send)
    wait_for(second.at[pl.ds(0, second.shape[0] - 1)], second_send)
    loss_copy.wait()
    wait_for(result.at[pl.ds(0, MEMBERS - 1)], res_send)
    wait_for(out, res_recv)


def local(prediction, reference_state, penalty, area, starts):
    rows, slots = prediction.shape[1:]
    tiles = slots // LANES
    share = rows // GROUPS
    spread = -(-(share + GROUPS - 1) // 8) * 8
    vmem = functools.partial(pltpu.VMEM, dtype=F32)
    array = functools.partial(jax.ShapeDtypeStruct, dtype=F32)
    dma = pltpu.SemaphoreType.DMA
    anywhere = pl.BlockSpec(memory_space=pl.ANY)
    fields = (MEMBERS, share, 8, LANES)
    edges = (SIDES, GROUPS, share, 8, LANES)
    runs = len(CHUNKS)
    y_share = (share + 1, 8, LANES)
    result, loss = pl.pallas_call(
        kernel,
        name="energy_score",
        out_shape=(pltpu.VMEM((rows, tiles // 2, LANES), F32), array((1, 1))),
        in_specs=[anywhere] * 5,
        out_specs=(anywhere, anywhere),
        scratch_shapes=[
            pltpu.SMEM(starts.shape, jnp.int32),
            pltpu.SMEM(penalty.shape, F32),
            vmem((1, 1)),
            vmem((GROUPS, share, tiles, LANES)),
            vmem((rows, slots)),
            vmem((tiles, LANES)),
            vmem(((spread + 1) * tiles, LANES)),
            vmem(edges),
            vmem(edges),
            vmem(fields),
            vmem(fields),
            vmem(y_share),
            vmem(y_share),
            vmem(y_share),
            vmem(fields),
            vmem((math.prod(AXES[a] for a in STAGES[0]), 1, LANES)),
            vmem((math.prod(AXES[a] for a in STAGES[1]), 1, LANES)),
            vmem((ENTRIES, 8, LANES)),
            dma((runs + 4,)),
            dma,
            dma((runs,)),
            dma,
            dma,
            dma,
            dma((runs,)),
            dma,
            dma,
            dma,
            dma,
            dma,
            dma,
            dma,
            pltpu.SemaphoreType.REGULAR((RELAYS,)),
        ],
        compiler_params=pltpu.CompilerParams(
            collective_id=0, has_side_effects=True, vmem_limit_bytes=VMEM_BYTES
        ),
    )(
        starts,
        penalty,
        prediction.reshape(GROUPS, share, tiles, LANES),
        reference_state,
        area.reshape(tiles, LANES),
    )
    return (result.reshape(1, rows, slots // 2), loss.reshape(()))


def solution(mesh):
    placed = (P("member", None, "grid"), P(None, "grid"), P(), P("grid"), P())
    return jax.shard_map(
        local,
        mesh=mesh,
        in_specs=placed,
        out_specs=(P("member", None, "grid"), P()),
        check_vma=False,
    )
```
